256 devices in a mesh: dp: 16 (over y, z_lo), block: 16 (over x, z_hi, core).
Axes of the slice: x: 4, y: 4, z: 8 (z_hi: 2, z_lo: 4; z = z_hi * 4 + z_lo), core: 2. Of those that a mesh axis runs over, the one named last changes fastest.
Arguments:
- grads: float32 [16, 16, 1024, 1024], P('dp', 'block'), may hold values from -0.15625 to 0.15625
- owner: int32 [16], replicated, may hold values from 0 to 15, as said below
- stats: float32 [16, 16, 512, 1024], P('block', 'dp'), as said below
Outputs:
- new_stats: float32 [16, 16, 512, 1024], P('block', 'dp')
- roots: float32 [16, 2, 1024, 1024], P('block', None, 'dp')
The draws below stay inside these ranges and needn't reach their ends.
Inputs may be any that keep to these rules, and one draw needn't show every extreme that they name: No owner has more than 4 blocks, and some owner has exactly 4. `stats`: each statistic matrix assembled from the row halves is symmetric.
All inputs are finite; a program needn't handle non-finite values.
Results may differ from the reference program's by a relative error of at most 0.0003.
Values sent between devices are 32-bit elements; how exact they have to be, the bound alone decides.
A program may use at most 128 MiB of HBM per device.

```python
import math
import jax
import jax.numpy as jnp
from jax import lax

BS = 1024
PSTEPS = 8
NB = 16
MAXB = 4
N_DP = 16
N_BLOCK = 16


def draw_owner(key, part):
    key = jax.random.fold_in(key, 3)
    key_heavy, key_slots, key_order = jax.random.split(key, 3)
    heavy_owner = jax.random.randint(key_heavy, (), 0, N_BLOCK, dtype=jnp.int32)
    slot_total = (N_BLOCK - 1) * MAXB
    last_first = (N_BLOCK - 2) * MAXB
    shuffled_slots = jax.random.permutation(key_slots, slot_total - 2).astype(jnp.int32)
    mapped_slots = shuffled_slots + 1
    mapped_slots = (mapped_slots + (mapped_slots >= last_first).astype(jnp.int32)).astype(jnp.int32)
    free_slots = jnp.concatenate([jnp.array([0, last_first], dtype=jnp.int32), mapped_slots[:NB - MAXB - 2]])
    others = (free_slots // MAXB).astype(jnp.int32)
    others = others + (others >= heavy_owner).astype(jnp.int32)
    assignment = jnp.concatenate([jnp.full((MAXB,), heavy_owner, dtype=jnp.int32), others])
    shuffled = jax.random.permutation(key_order, NB).astype(jnp.int32)
    return assignment[shuffled]


def draw_stats(key, part):
    key = jax.random.fold_in(key, 7)
    key_diag, key_off = jax.random.split(key, 2)
    diagonal_values = jnp.exp(jax.random.uniform(key_diag, (N_BLOCK, MAXB, 2, BS), jnp.float32, math.log(0.5), math.log(2.0)))
    noise = jax.random.uniform(key_off, (N_BLOCK, MAXB, 2, BS, BS), jnp.float32, -0.03, 0.03)
    symmetric = 0.5 * (noise + jnp.swapaxes(noise, -1, -2))
    identity = jnp.eye(BS, dtype=jnp.float32)
    matrix = symmetric * (1.0 - identity) + identity * diagonal_values[..., :, None]
    return matrix.reshape(N_BLOCK, N_DP, BS // 2, BS)


def strengthened(values, own_key, source, target, blocks, factor):
    def block_of(dim):
        return (jnp.arange(values.shape[dim]) // (values.shape[dim] // blocks)).reshape((-1,) + (1,) * (values.ndim - 1 - dim))

    near = jax.random.permutation(own_key, blocks)[block_of(target)]
    far = (block_of(target) + blocks // 2) % blocks
    return jnp.where((block_of(source) == near) | (block_of(source) == far), factor * values, values)


def levels(rng, extent, cuts, smallest, largest):
    gain = 1.0
    for position, blocks in cuts:
        heights = jax.random.uniform(jax.random.fold_in(jax.random.fold_in(rng, 6), position), (blocks,), jnp.float32, smallest / len(cuts), largest / len(cuts))
        gain = gain * jnp.repeat(jnp.exp(heights), extent[position] // blocks).reshape((-1,) + (1,) * (len(extent) - 1 - position))
    return gain


def noise_with(stream_key, dims, deviation, bound, pieces, heavy, kind=jnp.bfloat16):
    drawn = deviation * jax.random.normal(stream_key, dims, jnp.float32)
    if pieces:
        drawn = drawn * levels(stream_key, dims, pieces, -0.22, 0.18)
    return jnp.clip(strengthened(drawn, jax.random.fold_in(stream_key, 3), *heavy), -bound, bound).astype(kind)


def setup_inputs(seed: int = 0) -> dict:
    key_list = jax.random.split(jax.random.key(seed), 4)
    return {
        "grads": noise_with(key_list[0], (N_DP, NB, BS, BS), 0.008, 0.15625, ((0, 16), (1, 16)), (0, 2, 16, 2.0), jnp.float32),
        "owner": draw_owner(jax.random.fold_in(key_list[3], 71), 0),
        "stats": draw_stats(jax.random.fold_in(key_list[3], 71), 0),
    }


stat_decay = 0.6

def product(left_side, right_side):
    return jnp.dot(left_side, right_side, precision=lax.Precision.HIGHEST)

def inverse_root(statistic):
    probe = jnp.full((statistic.shape[0],), statistic.shape[0] ** (-0.5), dtype=statistic.dtype)
    for power_step in range(PSTEPS):
        image = product(statistic, probe)
        probe = image / jnp.sqrt(jnp.sum(image * image))
    final_image = product(statistic, probe)
    top_value = jnp.sqrt(jnp.sum(final_image * final_image))
    scale_value = 2.5 / top_value
    scaled = scale_value * statistic
    identity = jnp.eye(statistic.shape[0], dtype=statistic.dtype)
    first_step = (5.0 * identity - scaled) / 4.0
    iterate = first_step * scale_value ** 0.25
    square_term = product(first_step, first_step)
    fourth_term = product(square_term, square_term)
    updated = product(fourth_term, scaled)
    second_step = (5.0 * identity - updated) / 4.0
    return product(iterate, second_step)

def reference(grads, owner, stats):
    summed = lax.optimization_barrier(jnp.sum(grads, axis=0))
    block_ids = jnp.arange(NB, dtype=jnp.int32)
    slot_ids = jnp.arange(MAXB, dtype=jnp.int32)
    old_stats = stats.reshape(N_BLOCK, MAXB, 2, BS, BS)

    def per_owner(owner_id):
        owned_mask = (owner == owner_id).astype(jnp.int32)
        ranking = (jnp.cumsum(owned_mask) - 1).astype(jnp.int32)
        matched = (owned_mask[None, :] == 1) & (ranking[None, :] == slot_ids[:, None])
        chosen = lax.optimization_barrier(jnp.sum(jnp.where(matched, block_ids[None, :], 0), axis=1)).astype(jnp.int32)
        present = jnp.any(matched, axis=1)

        def per_slot(slot_id):
            gradient = summed[chosen[slot_id]] * present[slot_id].astype(summed.dtype)
            left_gram = product(gradient, gradient.T)
            right_gram = product(gradient.T, gradient)
            previous = old_stats[owner_id, slot_id]
            left_stat = stat_decay * previous[0] + (1.0 - stat_decay) * left_gram
            right_stat = stat_decay * previous[1] + (1.0 - stat_decay) * right_gram
            return (jnp.stack([left_stat, right_stat]), jnp.stack([inverse_root(left_stat), inverse_root(right_stat)]))
        return lax.map(per_slot, slot_ids)
    new_stats, slot_roots = lax.map(per_owner, jnp.arange(N_BLOCK, dtype=jnp.int32))
    same_owner = owner[None, :] == owner[:, None]
    earlier = block_ids[None, :] < block_ids[:, None]
    block_slot = lax.optimization_barrier(jnp.sum((same_owner & earlier).astype(jnp.int32), axis=1)).astype(jnp.int32)
    root_blocks = slot_roots[owner, block_slot]
    return (new_stats.reshape(N_BLOCK, N_DP, BS // 2, BS), root_blocks)
```

```python
import functools

import jax
import jax.numpy as jnp
from jax import lax
from jax.experimental import pallas as pl
from jax.experimental.pallas import tpu as pltpu
from jax.sharding import PartitionSpec as P

PSTEPS = 8
BS = 1024
HALVES = 2
SUB = 64 // HALVES
VMEM_LIMIT = 48 * 1024 * 1024

PACKED = (
    ((0, 0), (0, 1), (1, 1), (0, 2), (0, 3)),
    ((2, 2), (2, 3), (3, 3), (2, 1), (3, 1)),
)


def place(dp, block):
    return dp // 4, dp % 4, block // 4, block // 2 % 2, block % 2


def route(move):
    pairs = []
    for dp in range(16):
        for block in range(16):
            y, zl, x, zh, c = move(*place(dp, block))
            target = (y % 4 * 4 + zl % 4) * 16 + x % 4 * 4 + zh % 2 * 2 + c % 2
            pairs.append((dp * 16 + block, target))
    return pairs


def send(array, move):
    return lax.ppermute(array, ("dp", "block"), route(move))


def along_y(array, k):
    return send(array, lambda y, zl, x, zh, c: (y + k, zl, x, zh, c))


def along_z(array, k):
    return send(array, lambda y, zl, x, zh, c: (y, zl + k, x, zh, c))


def along_x(array, k):
    return send(array, lambda y, zl, x, zh, c: (y, zl, x + k, zh, c))


def across_z(array):
    return send(array, lambda y, zl, x, zh, c: (y, zl, x, zh + 1, c))


def across_core(array):
    return send(array, lambda y, zl, x, zh, c: (y, zl, x, zh, c + 1))


def across_half(array):
    return send(array, lambda y, zl, x, zh, c: (y, zl ^ 1, x, zh, c))


def across_side(array):
    return send(array, lambda y, zl, x, zh, c: (y, zl ^ 2, x, zh, c))


def pick(array, index, axis=0):
    return lax.dynamic_index_in_dim(array, index % 4, axis, keepdims=False)


def ring_gather(first, second, along):
    up_first = along(first, 1)
    down_second = along(second, -1)
    up_second = along(second, 1)
    down_first = along(first, -1)
    far_first = along(up_first, 1)
    far_second = along(down_second, -1)
    return [(first, second), (up_first, up_second), (far_first, far_second), (down_first, down_second)]


def reduce_part(part, y, zl):
    own, right, far, left = (pick(part, y + k) for k in range(4))
    far_up = along_y(far[:2], 1)
    far_down = along_y(far[2:], -1)
    up_second = along_y(right[2:], 1)
    down_first = along_y(left[:2], -1)
    up_first = along_y(right[:2] + far_up, 1)
    down_second = along_y(left[2:] + far_down, -1)
    mine = jnp.concatenate([own[:2] + up_first + down_first, own[2:] + up_second + down_second], axis=0)
    total = pick(mine, zl)
    for k in (1, 2, 3):
        total = total + along_z(pick(mine, zl + k), k)
    return total


def gather_part(total):
    pieces = [total] + [along_z(total, k) for k in (1, 2, 3)]
    return ring_gather(jnp.stack(pieces[:2]), jnp.stack(pieces[2:]), along_y)


def split(values):
    high = values.astype(jnp.bfloat16)
    return high, (values - high.astype(jnp.float32)).astype(jnp.bfloat16)


def gram_kernel(spot, *refs):
    y, zl, x = spot[0], spot[1], spot[2]
    side, half = zl // 2, zl % 2
    grads = refs[: 8 * HALVES]
    olds = refs[8 * HALVES : 8 * HALVES + 8]
    stat, piece, full, high, low = refs[8 * HALVES + 8 :]
    for part in range(HALVES):
        for k in range(4):
            for second in range(2):
                ref = grads[part * 8 + k * 2 + second]
                for n in range(2):
                    row = (y + 4 - k) % 4 * 256 + (zl + 4 - 2 * second - n) % 4 * 64 + part * SUB
                    row = pl.multiple_of(row, SUB)
                    values = ref[n]
                    full[pl.ds(row, SUB), :] = values
                    upper, lower = split(values)
                    high[pl.ds(row, SUB), :] = upper
                    low[pl.ds(row, SUB), :] = lower
    for k in range(4):
        for second in range(2):
            ref = olds[k * 2 + second]
            here = half if second == 0 else 1 - half
            for m in range(4):
                for n in range(5):
                    i = jnp.where(here == 0, PACKED[0][n][0], PACKED[1][n][0])
                    j = jnp.where(here == 0, PACKED[0][n][1], PACKED[1][n][1])
                    row = pl.multiple_of(i * 256 + (y + 4 - k) % 4 * 64 + (x + 4 - m) % 4 * 16, 16)
                    stat[pl.ds(row, 16), pl.ds(pl.multiple_of(j * 256, 256), 256)] = ref[m, n]
    for i, j in ((0, 1), (0, 2), (0, 3), (2, 1), (3, 1), (2, 3)):
        stat[pl.ds(j * 256, 256), pl.ds(i * 256, 256)] = stat[pl.ds(i * 256, 256), pl.ds(j * 256, 256)].T

    def finish(rows, gram):
        stat[rows, :] = 0.6 * stat[rows, :] + (1.0 - 0.6) * gram

    @pl.when(side == 0)
    def _():
        @pl.loop(0, 4)
        def _(i):
            rows = pl.ds(pl.multiple_of(i * 256, 256), 256)

            def product(a, b):
                return lax.dot_general(a, b, (((1,), (1,)), ((), ())), preferred_element_type=jnp.float32)

            finish(
                rows,
                product(high[rows, :], low[...])
                + product(low[rows, :], high[...])
                + product(high[rows, :], high[...]),
            )

    @pl.when(side == 1)
    def _():
        @pl.loop(0, 4)
        def _(i):
            rows = pl.ds(pl.multiple_of(i * 256, 256), 256)
            upper, lower = split(full[:, rows].T)

            def product(a, b):
                return jnp.dot(a, b, preferred_element_type=jnp.float32)

            finish(rows, product(upper, low[...]) + product(lower, high[...]) + product(upper, high[...]))

    for n in range(5):
        i = jnp.where(half == 0, PACKED[0][n][0], PACKED[1][n][0])
        j = jnp.where(half == 0, PACKED[0][n][1], PACKED[1][n][1])
        row = pl.multiple_of(i * 256 + y * 64, 64)
        piece[n] = stat[pl.ds(row, 64), pl.ds(pl.multiple_of(j * 256, 256), 256)]


def root_kernel(spot, stat, root, column, base, high, low):
    y, zl = spot[0], spot[1]

    def to_column(row):
        @pl.loop(0, 8)
        def _(i):
            rows = pl.ds(pl.multiple_of(i * 128, 128), 128)
            column[rows, :] = jnp.sum(stat[rows, :] * row, axis=1, keepdims=True)

        return column[...]

    def to_row(values):
        column[...] = values

        def body(i, total):
            rows = pl.ds(pl.multiple_of(i * 128, 128), 128)
            return total + jnp.sum(stat[rows, :] * column[rows, :], axis=0, keepdims=True)

        return lax.fori_loop(0, 8, body, jnp.zeros((1, BS), jnp.float32))

    row = jnp.full((1, BS), BS ** (-0.5), jnp.float32)
    for _ in range(PSTEPS // 2):
        image = to_column(row)
        image = image / jnp.sqrt(jnp.sum(image * image))
        row = to_row(image)
        row = row / jnp.sqrt(jnp.sum(row * row))
    image = to_column(row)
    top = jnp.sqrt(jnp.sum(image * image, axis=(0, 1), keepdims=True))
    scale = 2.5 / top
    fourth = jnp.sqrt(jnp.sqrt(scale))

    @pl.loop(0, 4)
    def _(i):
        rows = pl.ds(pl.multiple_of(i * 256, 256), 256)
        eye = lax.broadcasted_iota(jnp.int32, (256, BS), 0) + i * 256 == lax.broadcasted_iota(
            jnp.int32, (256, BS), 1
        )
        values = (jnp.where(eye, 5.0, 0.0) - scale * stat[rows, :]) / 4.0
        base[rows, :] = values
        upper, lower = split(values)
        high[rows, :] = upper
        low[rows, :] = lower

    def times(left):
        upper, lower = split(left)

        def product(a, b):
            return jnp.dot(a, b, preferred_element_type=jnp.float32)

        both = product(jnp.concatenate([upper, lower], axis=0), high[...])
        return both[128:] + product(upper, low[...]) + both[:128]

    own = pl.multiple_of((y * 4 + zl) * 64, 64)
    other = pl.multiple_of((y * 4 + (zl + 2) % 4) * 64, 64)
    first = jnp.concatenate([base[pl.ds(own, 64), :], base[pl.ds(other, 64), :]], axis=0)
    power = times(times(times(first)))
    result = (5.0 * first + times(4.0 * times(power) - 5.0 * power)) * (fourth / 4.0)
    root[0] = result[:64]
    root[1] = result[64:]


def finish_kernel(spot, *refs):
    y, half, present = spot[0], spot[1], spot[2]
    pieces, others = refs[:4], refs[4:8]
    old, new, packed, crossed = refs[8:]

    @pl.when(present == 0)
    def _():
        new[...] = 0.6 * old[...]

    @pl.when(present != 0)
    def _():
        for k in range(4):
            rows = pl.ds(pl.multiple_of((y + 4 - k) % 4 * 64, 64), 64)
            for n in range(5):
                packed[n, rows, :] = pieces[k][n]
            for n in range(2):
                crossed[n, rows, :] = others[k][n]

        def put(i, j, values):
            new[pl.ds(i * 256, 256), pl.ds(j * 256, 256)] = values

        @pl.when(half == 0)
        def _():
            put(0, 0, packed[0])
            put(0, 1, packed[1])
            put(0, 2, packed[3])
            put(0, 3, packed[4])
            put(1, 0, packed[1].T)
            put(1, 1, packed[2])
            put(1, 2, crossed[0].T)
            put(1, 3, crossed[1].T)

        @pl.when(half == 1)
        def _():
            put(0, 0, crossed[0].T)
            put(0, 1, packed[3])
            put(0, 2, packed[0])
            put(0, 3, packed[1])
            put(1, 0, crossed[1].T)
            put(1, 1, packed[4])
            put(1, 2, packed[1].T)
            put(1, 3, packed[2])


def local_call(kernel, out_shape, operands, scratch, flops, traffic):
    return pl.pallas_call(
        kernel,
        out_shape=out_shape,
        in_specs=[pl.BlockSpec(memory_space=pltpu.SMEM)]
        + [pl.BlockSpec(memory_space=pltpu.VMEM)] * (len(operands) - 1),
        out_specs=jax.tree.map(lambda _: pl.BlockSpec(memory_space=pltpu.VMEM), out_shape),
        scratch_shapes=scratch,
        cost_estimate=pl.CostEstimate(flops=flops, bytes_accessed=traffic, transcendentals=0),
        compiler_params=pltpu.CompilerParams(vmem_limit_bytes=VMEM_LIMIT),
    )(*operands)


def masked(entries, index, valid):
    taken = jnp.take(entries, jnp.where(valid, index, 0), axis=0, mode="clip")
    return jnp.where(valid.reshape((-1,) + (1,) * (taken.ndim - 1)), taken, 0.0)


def bring_old(old, owner, slot, y, x, zh, c, half):
    blocks = old.reshape(2, 256, 4, 256)
    upper = jnp.stack([blocks[i, :, j] for i, j in PACKED[0]])
    lower = jnp.stack([blocks[i - 2, :, j] for i, j in PACKED[1]])
    packed = jnp.where(half == 0, upper, lower).reshape(5, 4, 64, 256)
    slots = [pick(packed, y, 1)] + [along_y(pick(packed, y + k, 1), k) for k in (1, 2, 3)]
    slots = jnp.stack(slots).reshape(4, 5, 4, 16, 256)
    spread = [pick(slots, x, 2)] + [along_x(pick(slots, x + m, 2), m) for m in (1, 2, 3)]
    entries = jnp.stack(spread).reshape(16, 5, 16, 256)

    def chosen(core):
        u, m = jnp.meshgrid(jnp.arange(2), jnp.arange(4), indexing="ij")
        target = ((x + m) % 4 * 4 + (zh + u) % 2 * 2 + core).reshape(-1)
        source = owner[target]
        index = (x - source // 4) % 4 * 4 + (y - slot[target]) % 4
        return masked(entries, index, (source // 2 % 2 == zh) & (source % 2 == c))

    gathered = (across_core(chosen(1 - c)) + chosen(c)).reshape(2, 4, 5, 16, 256)
    near = gathered[0] + across_z(gathered[1])
    return jnp.stack([near[0]] + [along_x(near[m], m) for m in (1, 2, 3)])


def take_new(piece, owner, slot, y, x, zh, c):
    columns = ring_gather(piece, across_z(piece), along_x)
    entries = jnp.stack([part for pair in columns for part in pair])
    blocks = jnp.arange(16, dtype=jnp.int32)

    def chosen(core):
        column = x * 4 + zh * 2 + core
        wanted = (y + jnp.arange(4)) % 4
        matched = (owner == column)[None] & (slot[None] == wanted[:, None])
        source = jnp.sum(jnp.where(matched, blocks[None], 0), axis=1)
        index = (x - source // 4) % 4 * 2 + (source // 2 % 2 + zh) % 2
        return masked(entries, index, jnp.any(matched, axis=1) & (source % 2 == c))

    mine = across_core(chosen(1 - c)) + chosen(c)
    return [mine[0]] + [along_y(mine[k], k) for k in (1, 2, 3)]


def per_device(grads, owner, stats):
    dp, block = lax.axis_index("dp"), lax.axis_index("block")
    y, zl, x, zh, c = place(dp, block)
    side, half = zl // 2, zl % 2
    ids = jnp.arange(16, dtype=jnp.int32)
    slot = jnp.sum((owner[None] == owner[:, None]) & (ids[None] < ids[:, None]), axis=1, dtype=jnp.int32)
    old = stats[0, 0]

    parts = grads[0, 0].reshape(4, 4, HALVES, SUB, BS)
    totals = [reduce_part(parts[:, :, i], y, zl) for i in range(HALVES)]
    own_old = bring_old(old, owner, slot, y, x, zh, c, half)
    old_parts = ring_gather(own_old, across_half(own_old), along_y)
    grad_parts = [gather_part(total) for total in totals]

    spot = jnp.stack([y, zl, x]).astype(jnp.int32)
    operands = [spot]
    operands += [array for part in grad_parts for pair in part for array in pair]
    operands += [array for pair in old_parts for array in pair]
    stat, piece = local_call(
        gram_kernel,
        (jax.ShapeDtypeStruct((BS, BS), jnp.float32), jax.ShapeDtypeStruct((5, 64, 256), jnp.float32)),
        operands,
        [pltpu.VMEM((BS, BS), jnp.float32), pltpu.VMEM((BS, BS), jnp.bfloat16), pltpu.VMEM((BS, BS), jnp.bfloat16)],
        6 * BS**3,
        11 * 2**20,
    )
    root = local_call(
        root_kernel,
        jax.ShapeDtypeStruct((2, 64, BS), jnp.float32),
        [spot, stat],
        [
            pltpu.VMEM((BS, 1), jnp.float32),
            pltpu.VMEM((BS, BS), jnp.float32),
            pltpu.VMEM((BS, BS), jnp.bfloat16),
            pltpu.VMEM((BS, BS), jnp.bfloat16),
        ],
        20 * BS**3,
        4 * 2**20,
    )
    pieces = take_new(piece, owner, slot, y, x, zh, c)
    crossed = [across_half(part[3:]) for part in pieces]
    present = jnp.any((owner == block) & (slot == y))
    new = local_call(
        finish_kernel,
        jax.ShapeDtypeStruct((512, BS), jnp.float32),
        [jnp.stack([y, half, present.astype(jnp.int32)]).astype(jnp.int32), *pieces, *crossed, old],
        [pltpu.VMEM((5, 256, 256), jnp.float32), pltpu.VMEM((2, 256, 256), jnp.float32)],
        2**20,
        6 * 2**20,
    )
    other_root = across_side(root[1])
    left = jnp.where(side == 0, root[0], other_root)
    right = jnp.where(side == 0, other_root, root[0])
    return new[None, None], jnp.stack([left, right])[None]


def solution(mesh):
    return jax.shard_map(
        per_device,
        mesh=mesh,
        in_specs=(P("dp", "block", None, None), P(), P("block", "dp", None, None)),
        out_specs=(P("block", "dp", None, None), P("block", None, "dp", None)),
        check_vma=False,
    )
```

```python
import functools

import jax
import jax.numpy as jnp
from jax import lax
from jax.experimental import pallas as pl
from jax.experimental.pallas import tpu as pltpu
from jax.sharding import PartitionSpec as P

PSTEPS = 8
BS = 1024
GROUPS = 2
SUB = 64 // GROUPS
MESH = pl.DeviceIdType.MESH
VMEM_LIMIT = 48 * 1024 * 1024

PACKED = (
    ((0, 0), (0, 1), (1, 1), (0, 2), (0, 3)),
    ((2, 2), (2, 3), (3, 3), (2, 1), (3, 1)),
)


def place(dp, block):
    return dp // 4, dp % 4, block // 4, block // 2 % 2, block % 2


class Network:
    def __init__(self, send, recv, local):
        self.send, self.recv, self.local = send, recv, local
        self.count = self.locals = 0
        self.sent = []
        self.dp, self.block = lax.axis_index("dp"), lax.axis_index("block")
        self.y, self.zl, self.x, self.zh, self.c = place(self.dp, self.block)

    def device(self, y=0, zl=0, x=0, zh=0, c=0, half=0, side=0):
        row = (self.zl + zl) % 4
        if half:
            row = row + 1 - 2 * (row % 2)
        if side:
            row = (row + 2) % 4
        return (
            (self.y + y) % 4 * 4 + row,
            (self.x + x) % 4 * 4 + (self.zh + zh) % 2 * 2 + (self.c + c) % 2,
        )

    def greet(self, steps):
        barrier = pltpu.get_barrier_semaphore()
        for step in steps:
            pl.semaphore_signal(barrier, inc=1, device_id=self.device(**step), device_id_type=MESH)
        pl.semaphore_wait(barrier, len(steps))

    def push(self, source, target, **step):
        n = self.count
        self.count += 1
        copy = pltpu.make_async_remote_copy(
            src_ref=source,
            dst_ref=target,
            send_sem=self.send.at[n],
            recv_sem=self.recv.at[n],
            device_id=self.device(**step),
            device_id_type=MESH,
        )
        copy.start()
        self.sent.append(copy)
        return copy

    def move(self, source, target):
        copy = pltpu.make_async_copy(source, target, self.local.at[self.locals])
        self.locals += 1
        copy.start()
        return copy

    def close(self):
        for copy in self.sent:
            copy.wait_send()


def collect_kernel(index, valid, grads, old, total, olds, *scratch):
    (far, up, down, toward, away, home, stage, mine, zgot, ready) = scratch[:10]
    (packed, slots, spread, outgo, income, near, cross, fin) = scratch[10:18]
    net = Network(*scratch[18:])
    y, zl, x, zh, c = net.y, net.zl, net.x, net.zh, net.c
    half = zl % 2
    below, above, beyond = (y + 3) % 4, (y + 1) % 4, (y + 2) % 4

    def strip(ref, chunk, first, group):
        return ref.at[chunk, pl.ds(first, 2), pl.ds(group * SUB, SUB)]

    fetched = []
    for n in range(5):
        i = jnp.where(half == 0, PACKED[0][n][0], PACKED[1][n][0] - 2)
        j = jnp.where(half == 0, PACKED[0][n][1], PACKED[1][n][1])
        columns = pl.ds(pl.multiple_of(j * 256, 256), 256)
        fetched.append(net.move(old.at[pl.ds(pl.multiple_of(i * 256, 256), 256), columns], packed.at[n]))
    prefetch = [
        net.move(grads.at[above, pl.ds(0, 2)], toward),
        net.move(grads.at[below, pl.ds(2, 2)], away),
        net.move(grads.at[y], home),
    ]
    net.greet(
        [dict(y=1), dict(y=2), dict(y=3), dict(zl=1), dict(zl=2), dict(zl=3)]
        + [dict(x=1), dict(x=2), dict(x=3), dict(zh=1), dict(c=1)]
    )

    def scatter(group):
        far_up = net.push(strip(grads, beyond, 0, group), far.at[group, pl.ds(0, 2)], y=1)
        far_down = net.push(strip(grads, beyond, 2, group), far.at[group, pl.ds(2, 2)], y=3)
        near_up = net.push(strip(grads, above, 2, group), up.at[group, pl.ds(2, 2)], y=1)
        near_down = net.push(strip(grads, below, 0, group), down.at[group, pl.ds(0, 2)], y=3)
        return far_up, far_down, near_up, near_down

    def relay(group, copies):
        rows = pl.ds(group * SUB, SUB)
        copies[0].wait_recv()
        stage[group, 0:2] = far[group, 0:2] + toward[:, rows]
        first = net.push(stage.at[group, pl.ds(0, 2)], up.at[group, pl.ds(0, 2)], y=1)
        copies[1].wait_recv()
        stage[group, 2:4] = far[group, 2:4] + away[:, rows]
        second = net.push(stage.at[group, pl.ds(2, 2)], down.at[group, pl.ds(2, 2)], y=3)
        return first, second, copies[2], copies[3]

    def reduce_z(group, copies):
        for copy in copies:
            copy.wait_recv()
        mine[group] = home[:, pl.ds(group * SUB, SUB)] + up[group] + down[group]
        return [net.push(mine.at[group, (zl + k) % 4], zgot.at[group, k - 1], zl=k) for k in (1, 2, 3)]

    def gather_z(group, copies):
        for copy in copies:
            copy.wait_recv()
        ready[group] = mine[group, zl] + zgot[group, 0] + zgot[group, 1] + zgot[group, 2]
        here = total.at[y, zl, pl.ds(group * SUB, SUB)]
        kept = net.move(ready.at[group], here)
        return [net.push(ready.at[group], here, zl=k) for k in (1, 2, 3)], kept

    def gather_y(first, second):
        return (
            net.push(first(y), first(y), y=1),
            net.push(second(y), second(y), y=3),
            net.push(second(y), second(y), y=1),
            net.push(first(y), first(y), y=3),
        )

    def relay_y(first, second, copies):
        copies[0].wait_recv()
        one = net.push(first(below), first(below), y=1)
        copies[1].wait_recv()
        two = net.push(second(above), second(above), y=3)
        return one, two, copies[2], copies[3]

    def grad_parts(group):
        return (lambda at: strip(total, at, 0, group)), (lambda at: strip(total, at, 2, group))

    scattered = scatter(0)
    for copy in fetched:
        copy.wait()
    own_slot = net.move(packed.at[:, pl.ds(pl.multiple_of(y * 64, 64), 64)], slots.at[y])
    slotted = {}
    for k in (1, 3, 2):
        rows = pl.ds(pl.multiple_of((y + k) % 4 * 64, 64), 64)
        slotted[k] = net.push(packed.at[:, rows], slots.at[y], y=k)
    for copy in prefetch:
        copy.wait()
    relayed = relay(0, scattered)
    scattered = scatter(1)

    spreads = []
    for k in (0, 1, 3, 2):
        if k == 0:
            own_slot.wait()
        else:
            slotted[k].wait_recv()
        at = (y + 4 - k) % 4
        for m in (0, 1, 2, 3):
            source = slots.at[at, :, pl.ds(pl.multiple_of((x + m) % 4 * 16, 16), 16)]
            if m == 0:
                spreads.append(net.move(source, spread.at[x * 4 + at]))
            else:
                spreads.append(net.push(source, spread.at[x * 4 + at], x=m))
    reduced = reduce_z(0, relayed)
    relayed = relay(1, scattered)

    for n, copy in enumerate(spreads):
        if n % 4:
            copy.wait_recv()
        else:
            copy.wait()
    for n in range(8):
        outgo[n] = spread[index[8 + n]] * valid[8 + n]
    swapped = net.push(outgo, income, c=1)
    for n in range(8):
        near[n] = spread[index[n]] * valid[n]
    gathered, kept = gather_z(0, reduced)
    swapped.wait_recv()
    for n in range(8):
        near[n] = near[n] + income[n]
    crossed = net.push(near.at[pl.ds(4, 4)], cross, zh=1)
    reduced = reduce_z(1, relayed)
    kept.wait()
    for copy in gathered:
        copy.wait_recv()
    first, second = grad_parts(0)
    rung = gather_y(first, second)
    crossed.wait_recv()
    for n in range(4):
        fin[n] = near[n] + cross[n]
    place_here = olds.at[half, :, y, pl.ds(pl.multiple_of(x * 16, 16), 16)]
    own_old = net.move(fin.at[0], place_here)
    brought = [net.push(fin.at[m], place_here, x=m) for m in (1, 2, 3)]
    gathered, kept = gather_z(1, reduced)
    own_old.wait()
    for copy in brought:
        copy.wait_recv()

    def old_first(at):
        return olds.at[half, :, at]

    def old_second(at):
        return olds.at[1 - half, :, at]

    halved = net.push(old_first(y), old_first(y), half=1)
    rung = relay_y(first, second, rung)
    halved.wait_recv()
    old_rung = gather_y(old_first, old_second)
    kept.wait()
    for copy in gathered:
        copy.wait_recv()
    first, second = grad_parts(1)
    last_rung = gather_y(first, second)
    old_rung = relay_y(old_first, old_second, old_rung)
    last_rung = relay_y(first, second, last_rung)
    for copy in rung + old_rung + last_rung:
        copy.wait_recv()
    net.close()


def deliver_kernel(index, valid, piece, root, parts, crossed, other_root, *scratch):
    columns, outgo, income, ready = scratch[:4]
    net = Network(*scratch[4:])
    y, zl, x, zh = net.y, net.zl, net.x, net.zh
    net.greet(
        [dict(y=1), dict(y=2), dict(y=3), dict(x=1), dict(x=3), dict(zh=1), dict(c=1), dict(half=1), dict(side=1)]
    )
    here = columns.at[x * 2 + zh]
    own = net.move(piece, here)
    across = net.push(piece, here, zh=1)
    first_up = net.push(piece, here, x=1)
    first_down = net.push(piece, here, x=3)
    returned = net.push(root.at[1], other_root, side=1)
    back, on = (x + 3) % 4, (x + 1) % 4
    first_up.wait_recv()
    there = columns.at[back * 2 + zh]
    first_far = net.push(there, there, x=1)
    across.wait_recv()
    here = columns.at[x * 2 + 1 - zh]
    second_down = net.push(here, here, x=3)
    second_up = net.push(here, here, x=1)
    second_down.wait_recv()
    there = columns.at[on * 2 + 1 - zh]
    second_far = net.push(there, there, x=3)
    own.wait()
    for copy in (first_down, first_far, second_up, second_far):
        copy.wait_recv()
    swapped = {}
    for k in (2, 1, 3, 0):
        outgo[k] = columns[index[4 + k]] * valid[4 + k]
        swapped[k] = net.push(outgo.at[k], income.at[k], c=1)
    sent = {}
    for k in (2, 1, 3, 0):
        ready[k] = columns[index[k]] * valid[k]
        swapped[k].wait_recv()
        ready[k] = ready[k] + income[k]
        if k:
            sent[k] = net.push(ready.at[k], parts.at[:, y], y=k)
        else:
            own = net.move(ready.at[0], parts.at[:, y])
    own.wait()
    halves = []
    for k in (0, 1, 3, 2):
        if k:
            sent[k].wait_recv()
        at = (y + 4 - k) % 4
        halves.append(net.push(parts.at[pl.ds(3, 2), at], crossed.at[:, at], half=1))
    for copy in halves:
        copy.wait_recv()
    returned.wait_recv()
    net.close()


def remote_call(kernel, tables, operands, out_shape, scratch, copies, locals_, collective_id):
    return pl.pallas_call(
        kernel,
        out_shape=out_shape,
        in_specs=[pl.BlockSpec(memory_space=pltpu.SMEM)] * 2
        + [pl.BlockSpec(memory_space=pl.ANY)] * len(operands),
        out_specs=jax.tree.map(lambda _: pl.BlockSpec(memory_space=pl.ANY), out_shape),
        scratch_shapes=[pltpu.VMEM(shape, jnp.float32) for shape in scratch]
        + [
            pltpu.SemaphoreType.DMA((copies,)),
            pltpu.SemaphoreType.DMA((copies,)),
            pltpu.SemaphoreType.DMA((locals_,)),
        ],
        compiler_params=pltpu.CompilerParams(
            collective_id=collective_id, has_side_effects=True, vmem_limit_bytes=VMEM_LIMIT
        ),
    )(*tables, *operands)


def split(values):
    high = values.astype(jnp.bfloat16)
    return high, (values - high.astype(jnp.float32)).astype(jnp.bfloat16)


def gram_kernel(spot, full, olds, stat, piece, high, low):
    y, zl = spot[0], spot[1]
    side, half = zl // 2, zl % 2
    high[...], low[...] = split(full[...])
    for h in range(2):
        for n in range(5):
            i, j = PACKED[h][n]
            stat[pl.ds(i * 256, 256), pl.ds(j * 256, 256)] = olds[h, n]
    for i, j in ((0, 1), (0, 2), (0, 3), (2, 1), (3, 1), (2, 3)):
        stat[pl.ds(j * 256, 256), pl.ds(i * 256, 256)] = stat[pl.ds(i * 256, 256), pl.ds(j * 256, 256)].T

    def finish(rows, gram):
        stat[rows, :] = 0.6 * stat[rows, :] + (1.0 - 0.6) * gram

    @pl.when(side == 0)
    def _():
        @pl.loop(0, 4)
        def _(i):
            rows = pl.ds(pl.multiple_of(i * 256, 256), 256)

            def product(a, b):
                return lax.dot_general(a, b, (((1,), (1,)), ((), ())), preferred_element_type=jnp.float32)

            finish(
                rows,
                product(high[rows, :], low[...])
                + product(low[rows, :], high[...])
                + product(high[rows, :], high[...]),
            )

    @pl.when(side == 1)
    def _():
        @pl.loop(0, 4)
        def _(i):
            rows = pl.ds(pl.multiple_of(i * 256, 256), 256)
            upper, lower = split(full[:, rows].T)

            def product(a, b):
                return jnp.dot(a, b, preferred_element_type=jnp.float32)

            finish(rows, product(upper, low[...]) + product(lower, high[...]) + product(upper, high[...]))

    for n in range(5):
        i = jnp.where(half == 0, PACKED[0][n][0], PACKED[1][n][0])
        j = jnp.where(half == 0, PACKED[0][n][1], PACKED[1][n][1])
        row = pl.multiple_of(i * 256 + y * 64, 64)
        piece[n] = stat[pl.ds(row, 64), pl.ds(pl.multiple_of(j * 256, 256), 256)]


def root_kernel(spot, stat, root, column, base, high, low):
    y, zl = spot[0], spot[1]

    def to_column(row):
        @pl.loop(0, 8)
        def _(i):
            rows = pl.ds(pl.multiple_of(i * 128, 128), 128)
            column[rows, :] = jnp.sum(stat[rows, :] * row, axis=1, keepdims=True)

        return column[...]

    def to_row(values):
        column[...] = values

        def body(i, total):
            rows = pl.ds(pl.multiple_of(i * 128, 128), 128)
            return total + jnp.sum(stat[rows, :] * column[rows, :], axis=0, keepdims=True)

        return lax.fori_loop(0, 8, body, jnp.zeros((1, BS), jnp.float32))

    row = jnp.full((1, BS), BS ** (-0.5), jnp.float32)
    for _ in range(PSTEPS // 2):
        image = to_column(row)
        image = image / jnp.sqrt(jnp.sum(image * image))
        row = to_row(image)
        row = row / jnp.sqrt(jnp.sum(row * row))
    image = to_column(row)
    top = jnp.sqrt(jnp.sum(image * image, axis=(0, 1), keepdims=True))
    scale = 2.5 / top
    fourth = jnp.sqrt(jnp.sqrt(scale))

    @pl.loop(0, 4)
    def _(i):
        rows = pl.ds(pl.multiple_of(i * 256, 256), 256)
        eye = lax.broadcasted_iota(jnp.int32, (256, BS), 0) + i * 256 == lax.broadcasted_iota(
            jnp.int32, (256, BS), 1
        )
        values = (jnp.where(eye, 5.0, 0.0) - scale * stat[rows, :]) / 4.0
        base[rows, :] = values
        upper, lower = split(values)
        high[rows, :] = upper
        low[rows, :] = lower

    def times(left):
        upper, lower = split(left)

        def product(a, b):
            return jnp.dot(a, b, preferred_element_type=jnp.float32)

        both = product(jnp.concatenate([upper, lower], axis=0), high[...])
        return both[128:] + product(upper, low[...]) + both[:128]

    own = pl.multiple_of((y * 4 + zl) * 64, 64)
    other = pl.multiple_of((y * 4 + (zl + 2) % 4) * 64, 64)
    first = jnp.concatenate([base[pl.ds(own, 64), :], base[pl.ds(other, 64), :]], axis=0)
    power = times(times(times(first)))
    result = (5.0 * first + times(4.0 * times(power) - 5.0 * power)) * (fourth / 4.0)
    root[0] = result[:64]
    root[1] = result[64:]


def finish_kernel(spot, packed, crossed, old, new):
    half, present = spot[0], spot[1]

    @pl.when(present == 0)
    def _():
        new[...] = 0.6 * old[...]

    @pl.when(present != 0)
    def _():
        def put(i, j, values):
            new[pl.ds(i * 256, 256), pl.ds(j * 256, 256)] = values

        @pl.when(half == 0)
        def _():
            put(0, 0, packed[0])
            put(0, 1, packed[1])
            put(0, 2, packed[3])
            put(0, 3, packed[4])
            put(1, 0, packed[1].T)
            put(1, 1, packed[2])
            put(1, 2, crossed[0].T)
            put(1, 3, crossed[1].T)

        @pl.when(half == 1)
        def _():
            put(0, 0, crossed[0].T)
            put(0, 1, packed[3])
            put(0, 2, packed[0])
            put(0, 3, packed[1])
            put(1, 0, crossed[1].T)
            put(1, 1, packed[4])
            put(1, 2, packed[1].T)
            put(1, 3, packed[2])


def local_call(kernel, out_shape, operands, scratch, flops, traffic):
    return pl.pallas_call(
        kernel,
        out_shape=out_shape,
        in_specs=[pl.BlockSpec(memory_space=pltpu.SMEM)]
        + [pl.BlockSpec(memory_space=pltpu.VMEM)] * (len(operands) - 1),
        out_specs=jax.tree.map(lambda _: pl.BlockSpec(memory_space=pltpu.VMEM), out_shape),
        scratch_shapes=scratch,
        cost_estimate=pl.CostEstimate(flops=flops, bytes_accessed=traffic, transcendentals=0),
        compiler_params=pltpu.CompilerParams(vmem_limit_bytes=VMEM_LIMIT),
    )(*operands)


def bring_tables(owner, slot, y, x, zh, c):
    u, m = jnp.meshgrid(jnp.arange(2), jnp.arange(4), indexing="ij")
    target = (x + m) % 4 * 4 + (zh + u) % 2 * 2
    target = jnp.concatenate([(target + c).reshape(-1), (target + 1 - c).reshape(-1)])
    source = owner[target]
    valid = (source // 2 % 2 == zh) & (source % 2 == c)
    index = source // 4 * 4 + slot[target]
    return jnp.where(valid, index, 0).astype(jnp.int32), valid.astype(jnp.float32)


def take_tables(owner, slot, y, x, zh, c):
    columns = jnp.repeat(x * 4 + zh * 2 + jnp.stack([c, 1 - c]), 4)
    wanted = jnp.tile((y + jnp.arange(4)) % 4, 2)
    matched = (owner[None] == columns[:, None]) & (slot[None] == wanted[:, None])
    source = jnp.sum(jnp.where(matched, jnp.arange(16, dtype=jnp.int32)[None], 0), axis=1)
    valid = jnp.any(matched, axis=1) & (source % 2 == c)
    return jnp.where(valid, source // 2, 0).astype(jnp.int32), valid.astype(jnp.float32)


def f32(*shape):
    return jax.ShapeDtypeStruct(shape, jnp.float32)


def per_device(grads, owner, stats):
    dp, block = lax.axis_index("dp"), lax.axis_index("block")
    y, zl, x, zh, c = place(dp, block)
    side, half = zl // 2, zl % 2
    ids = jnp.arange(16, dtype=jnp.int32)
    slot = jnp.sum((owner[None] == owner[:, None]) & (ids[None] < ids[:, None]), axis=1, dtype=jnp.int32)
    old = stats[0, 0]
    strips = (GROUPS, 4, SUB, BS)
    total, olds = remote_call(
        collect_kernel,
        bring_tables(owner, slot, y, x, zh, c),
        [grads.reshape(4, 4, 64, BS), old],
        (f32(4, 4, 64, BS), f32(2, 5, 4, 64, 256)),
        [strips, strips, strips, (2, 64, BS), (2, 64, BS), (4, 64, BS), strips, strips]
        + [(GROUPS, 3, SUB, BS), (GROUPS, SUB, BS)]
        + [(5, 256, 256), (4, 5, 64, 256), (16, 5, 16, 256)]
        + [(8, 5, 16, 256), (8, 5, 16, 256), (8, 5, 16, 256), (4, 5, 16, 256), (4, 5, 16, 256)],
        64,
        16,
        0,
    )
    spot = jnp.stack([y, zl]).astype(jnp.int32)
    stat, piece = local_call(
        gram_kernel,
        (f32(BS, BS), f32(5, 64, 256)),
        [spot, total.reshape(BS, BS), olds.reshape(2, 5, 256, 256)],
        [pltpu.VMEM((BS, BS), jnp.bfloat16), pltpu.VMEM((BS, BS), jnp.bfloat16)],
        6 * BS**3,
        11 * 2**20,
    )
    root = local_call(
        root_kernel,
        f32(2, 64, BS),
        [spot, stat],
        [
            pltpu.VMEM((BS, 1), jnp.float32),
            pltpu.VMEM((BS, BS), jnp.float32),
            pltpu.VMEM((BS, BS), jnp.bfloat16),
            pltpu.VMEM((BS, BS), jnp.bfloat16),
        ],
        20 * BS**3,
        4 * 2**20,
    )
    parts, crossed, other_root = remote_call(
        deliver_kernel,
        take_tables(owner, slot, y, x, zh, c),
        [piece, root],
        (f32(5, 4, 64, 256), f32(2, 4, 64, 256), f32(64, BS)),
        [(8, 5, 64, 256), (4, 5, 64, 256), (4, 5, 64, 256), (4, 5, 64, 256)],
        24,
        2,
        1,
    )
    present = jnp.any((owner == block) & (slot == y))
    new = local_call(
        finish_kernel,
        f32(512, BS),
        [
            jnp.stack([half, present.astype(jnp.int32)]).astype(jnp.int32),
            parts.reshape(5, 256, 256),
            crossed.reshape(2, 256, 256),
            old,
        ],
        [],
        2**20,
        6 * 2**20,
    )
    left = jnp.where(side == 0, root[0], other_root)
    right = jnp.where(side == 0, other_root, root[0])
    return new[None, None], jnp.stack([left, right])[None]


def solution(mesh):
    return jax.shard_map(
        per_device,
        mesh=mesh,
        in_specs=(P("dp", "block", None, None), P(), P("block", "dp", None, None)),
        out_specs=(P("block", "dp", None, None), P("block", None, "dp", None)),
        check_vma=False,
    )
```

```python
import jax
import jax.numpy as jnp
from jax import lax
from jax.experimental import pallas as pl
from jax.experimental.pallas import tpu as pltpu
from jax.sharding import PartitionSpec as P

PSTEPS = 8
BS = 1024
GROUPS = 2
SUB = 64 // GROUPS
MESH = pl.DeviceIdType.MESH
VMEM_LIMIT = 60 * 1024 * 1024

PACKED = (
    ((0, 0), (0, 1), (1, 1), (0, 2), (0, 3)),
    ((2, 2), (2, 3), (3, 3), (2, 1), (3, 1)),
)


def place(dp, block):
    return dp // 4, dp % 4, block // 4, block // 2 % 2, block % 2


class Network:
    def __init__(self, send, recv, local):
        self.send, self.recv, self.local = send, recv, local
        self.count = self.locals = 0
        self.sent = []
        self.dp, self.block = lax.axis_index("dp"), lax.axis_index("block")
        self.y, self.zl, self.x, self.zh, self.c = place(self.dp, self.block)

    def device(self, y=0, zl=0, x=0, zh=0, c=0, half=0, side=0):
        row = (self.zl + zl) % 4
        if half:
            row = row + 1 - 2 * (row % 2)
        if side:
            row = (row + 2) % 4
        return (
            (self.y + y) % 4 * 4 + row,
            (self.x + x) % 4 * 4 + (self.zh + zh) % 2 * 2 + (self.c + c) % 2,
        )

    def greet(self, steps):
        barrier = pltpu.get_barrier_semaphore()
        for step in steps:
            pl.semaphore_signal(barrier, inc=1, device_id=self.device(**step), device_id_type=MESH)
        pl.semaphore_wait(barrier, len(steps))

    def push(self, source, target, **step):
        n = self.count
        self.count += 1
        copy = pltpu.make_async_remote_copy(
            src_ref=source,
            dst_ref=target,
            send_sem=self.send.at[n],
            recv_sem=self.recv.at[n],
            device_id=self.device(**step),
            device_id_type=MESH,
        )
        copy.start()
        self.sent.append(copy)
        return copy

    def move(self, source, target):
        copy = pltpu.make_async_copy(source, target, self.local.at[self.locals])
        self.locals += 1
        copy.start()
        return copy

    def close(self):
        for copy in self.sent:
            copy.wait_send()


def split(values):
    high = values.astype(jnp.bfloat16)
    return high, (values - high.astype(jnp.float32)).astype(jnp.bfloat16)


def rank_of(owner, block):
    mine = owner[block]
    count = lax.fori_loop(
        0, 16, lambda i, n: n + jnp.where((i < block) & (owner[i] == mine), 1, 0), jnp.int32(0)
    )
    return mine, count


def block_at(owner, column, wanted):
    def step(i, carry):
        count, found, source = carry
        hit = owner[i] == column
        here = hit & (count == wanted)
        return count + jnp.where(hit, 1, 0), jnp.where(here, 1, found), jnp.where(here, i, source)

    zero = jnp.int32(0)
    _, found, source = lax.fori_loop(0, 16, step, (zero, zero, zero))
    return found, source


def find_root(spot, stat, root, column, base, high, low):
    y, zl = spot

    def to_column(row):
        @pl.loop(0, 8)
        def _(i):
            rows = pl.ds(pl.multiple_of(i * 128, 128), 128)
            column[rows, :] = jnp.sum(stat[rows, :] * row, axis=1, keepdims=True)

        return column[...]

    def to_row(values):
        column[...] = values

        def body(i, total):
            rows = pl.ds(pl.multiple_of(i * 128, 128), 128)
            return total + jnp.sum(stat[rows, :] * column[rows, :], axis=0, keepdims=True)

        return lax.fori_loop(0, 8, body, jnp.zeros((1, BS), jnp.float32))

    row = jnp.full((1, BS), BS ** (-0.5), jnp.float32)
    for _ in range(PSTEPS // 2):
        image = to_column(row)
        image = image / jnp.sqrt(jnp.sum(image * image))
        row = to_row(image)
        row = row / jnp.sqrt(jnp.sum(row * row))
    image = to_column(row)
    top = jnp.sqrt(jnp.sum(image * image, axis=(0, 1), keepdims=True))
    scale = 2.5 / top
    fourth = jnp.sqrt(jnp.sqrt(scale))

    @pl.loop(0, 4)
    def _(i):
        rows = pl.ds(pl.multiple_of(i * 256, 256), 256)
        eye = lax.broadcasted_iota(jnp.int32, (256, BS), 0) + i * 256 == lax.broadcasted_iota(
            jnp.int32, (256, BS), 1
        )
        values = (jnp.where(eye, 5.0, 0.0) - scale * stat[rows, :]) / 4.0
        base[rows, :] = values
        upper, lower = split(values)
        high[rows, :] = upper
        low[rows, :] = lower

    def times(left):
        upper, lower = split(left)

        def product(a, b):
            return jnp.dot(a, b, preferred_element_type=jnp.float32)

        both = product(jnp.concatenate([upper, lower], axis=0), high[...])
        return both[128:] + product(upper, low[...]) + both[:128]

    own = pl.multiple_of((y * 4 + zl) * 64, 64)
    other = pl.multiple_of((y * 4 + (zl + 2) % 4) * 64, 64)
    first = jnp.concatenate([base[pl.ds(own, 64), :], base[pl.ds(other, 64), :]], axis=0)
    power = times(times(times(first)))
    result = (5.0 * first + times(4.0 * times(power) - 5.0 * power)) * (fourth / 4.0)
    root[0] = result[:64]
    root[1] = result[64:]


def refresh_kernel(owner, grads, old, parts, crossed, roots, *scratch):
    (far, up, down, toward, away, home, stage, mine, zgot) = scratch[:9]
    (packed, slots, spread, outgo, income, near, cross, fin, oldp) = scratch[9:18]
    (both, chunk, gram, ggot, sall, stat, column, base, rootbuf) = scratch[18:27]
    (columns, leave, enter, ready, piece) = scratch[27:32]
    (mat_high, mat_low, high, low) = scratch[32:36]
    net = Network(*scratch[36:])
    y, zl, x, zh, c = net.y, net.zl, net.x, net.zh, net.c
    side, half = zl // 2, zl % 2
    below, above, beyond = (y + 3) % 4, (y + 1) % 4, (y + 2) % 4

    def rows_of(at, size):
        return pl.ds(pl.multiple_of(at * size, size), size)

    def strip(ref, chunk_at, first, group):
        return ref.at[chunk_at, pl.ds(first, 2), pl.ds(group * SUB, SUB)]

    fetched = []
    for n in range(5):
        i = jnp.where(half == 0, PACKED[0][n][0], PACKED[1][n][0] - 2)
        j = jnp.where(half == 0, PACKED[0][n][1], PACKED[1][n][1])
        fetched.append(net.move(old.at[rows_of(i, 256), rows_of(j, 256)], packed.at[n]))
    prefetch = [
        net.move(grads.at[above, pl.ds(0, 2)], toward),
        net.move(grads.at[below, pl.ds(2, 2)], away),
        net.move(grads.at[y], home),
    ]
    net.greet(
        [dict(y=1), dict(y=2), dict(y=3), dict(zl=1), dict(zl=2), dict(zl=3)]
        + [dict(x=1), dict(x=2), dict(x=3), dict(zh=1), dict(c=1)]
    )

    def scatter(group):
        far_up = net.push(strip(grads, beyond, 0, group), far.at[group, pl.ds(0, 2)], y=1)
        far_down = net.push(strip(grads, beyond, 2, group), far.at[group, pl.ds(2, 2)], y=3)
        near_up = net.push(strip(grads, above, 2, group), up.at[group, pl.ds(2, 2)], y=1)
        near_down = net.push(strip(grads, below, 0, group), down.at[group, pl.ds(0, 2)], y=3)
        return far_up, far_down, near_up, near_down

    def relay(group, copies):
        rows = pl.ds(group * SUB, SUB)
        copies[0].wait_recv()
        stage[group, 0:2] = far[group, 0:2] + toward[:, rows]
        first = net.push(stage.at[group, pl.ds(0, 2)], up.at[group, pl.ds(0, 2)], y=1)
        copies[1].wait_recv()
        stage[group, 2:4] = far[group, 2:4] + away[:, rows]
        second = net.push(stage.at[group, pl.ds(2, 2)], down.at[group, pl.ds(2, 2)], y=3)
        return first, second, copies[2], copies[3]

    def reduce_z(group, copies):
        for copy in copies:
            copy.wait_recv()
        mine[group] = home[:, pl.ds(group * SUB, SUB)] + up[group] + down[group]
        return [net.push(mine.at[group, (zl + k) % 4], zgot.at[group, k - 1], zl=k) for k in (1, 2, 3)]

    def turn(group, copies):
        for copy in copies:
            copy.wait_recv()
        total = mine[group, zl] + zgot[group, 0] + zgot[group, 1] + zgot[group, 2]
        for a in range(4):
            both[1, group, a] = total[:, a * 256 : (a + 1) * 256]
        kept = net.move(both.at[1, group, y], both.at[0, group, y])
        return [net.push(both.at[1, group, (y + k) % 4], both.at[0, group, y], y=k) for k in (1, 3, 2)], kept

    def gather_z(group, turned):
        copies, kept = turned
        for copy in copies:
            copy.wait_recv()
        kept.wait()
        here = chunk.at[:, zl, pl.ds(group * SUB, SUB)]
        kept = net.move(both.at[side, group], here)
        return [net.push(both.at[(zl + k) % 4 // 2, group], here, zl=k) for k in (1, 2, 3)], kept

    scattered = scatter(0)
    for copy in fetched:
        copy.wait()
    own_slot = net.move(packed.at[:, rows_of(y, 64)], slots.at[y])
    slotted = {k: net.push(packed.at[:, rows_of((y + k) % 4, 64)], slots.at[y], y=k) for k in (1, 3, 2)}
    for copy in prefetch:
        copy.wait()
    relayed = relay(0, scattered)
    scattered = scatter(1)

    spreads = []
    for k in (0, 1, 3, 2):
        if k == 0:
            own_slot.wait()
        else:
            slotted[k].wait_recv()
        at = (y + 4 - k) % 4
        for m in (0, 1, 2, 3):
            source = slots.at[at, :, rows_of((x + m) % 4, 16)]
            if m == 0:
                spreads.append(net.move(source, spread.at[x * 4 + at]))
            else:
                spreads.append(net.push(source, spread.at[x * 4 + at], x=m))
    reduced = reduce_z(0, relayed)
    relayed = relay(1, scattered)

    for n, copy in enumerate(spreads):
        if n % 4:
            copy.wait_recv()
        else:
            copy.wait()

    def chosen(n, core):
        target = (x + n % 4) % 4 * 4 + (zh + n // 4) % 2 * 2 + core
        source, slot = rank_of(owner, target)
        valid = (source // 2 % 2 == zh) & (source % 2 == c)
        values = spread[jnp.where(valid, source // 4 * 4 + slot, 0)]
        return values * jnp.where(valid, 1.0, 0.0)

    for n in range(8):
        outgo[n] = chosen(n, 1 - c)
    swapped = net.push(outgo, income, c=1)
    for n in range(8):
        near[n] = chosen(n, c)
    turned = turn(0, reduced)
    swapped.wait_recv()
    for n in range(8):
        near[n] = near[n] + income[n]
    crossing = net.push(near.at[pl.ds(4, 4)], cross, zh=1)
    reduced = reduce_z(1, relayed)
    gathered, first_kept = gather_z(0, turned)
    turned = turn(1, reduced)
    crossing.wait_recv()
    for n in range(4):
        fin[n] = near[n] + cross[n]
    place_here = oldp.at[:, rows_of(x, 16)]
    own_old = net.move(fin.at[0], place_here)
    brought = [net.push(fin.at[m], place_here, x=m) for m in (1, 2, 3)]
    more, second_kept = gather_z(1, turned)
    for copy in gathered + more:
        copy.wait_recv()
    first_kept.wait()
    second_kept.wait()

    @pl.when(side == 1)
    def _():
        for a in range(4):
            mat_high[a], mat_low[a] = split(chunk[a].reshape(256, 256).T)

    @pl.when(side == 0)
    def _():
        for a in range(4):
            mat_high[a], mat_low[a] = split(chunk[a].reshape(256, 256))

    def outer(a, b):
        return lax.dot_general(a, b, (((1,), (1,)), ((), ())), preferred_element_type=jnp.float32)

    for n in range(5):
        i = jnp.where(half == 0, PACKED[0][n][0], PACKED[1][n][0])
        j = jnp.where(half == 0, PACKED[0][n][1], PACKED[1][n][1])
        left_high, right_high = mat_high[i], mat_high[j]
        gram[n] = (
            outer(left_high, mat_low[j]) + outer(mat_low[i], right_high) + outer(left_high, right_high)
        )
    summed = [net.push(gram.at[:, rows_of((y + k) % 4, 64)], ggot.at[k - 1], y=k) for k in (1, 3, 2)]
    own_old.wait()
    for copy in brought + summed:
        copy.wait_recv()
    piece[...] = 0.6 * oldp[...] + (1.0 - 0.6) * (gram[:, rows_of(y, 64)] + ggot[0] + ggot[1] + ggot[2])

    here = columns.at[x * 2 + zh]
    there = sall.at[half, :, y]
    own = net.move(piece, here)
    own_piece = net.move(piece, there)
    across = net.push(piece, here, zh=1)
    first_up = net.push(piece, here, x=1)
    first_down = net.push(piece, here, x=3)
    halved = net.push(piece, there, half=1)
    y_up = net.push(piece, there, y=1)
    y_down = net.push(piece, there, y=3)
    back, on = (x + 3) % 4, (x + 1) % 4
    first_up.wait_recv()
    there = columns.at[back * 2 + zh]
    first_far = net.push(there, there, x=1)
    y_up.wait_recv()
    there = sall.at[half, :, below]
    y_far = net.push(there, there, y=1)
    halved.wait_recv()
    there = sall.at[1 - half, :, y]
    other_down = net.push(there, there, y=3)
    other_up = net.push(there, there, y=1)
    across.wait_recv()
    there = columns.at[x * 2 + 1 - zh]
    second_down = net.push(there, there, x=3)
    second_up = net.push(there, there, x=1)
    other_down.wait_recv()
    there = sall.at[1 - half, :, above]
    other_far = net.push(there, there, y=3)
    second_down.wait_recv()
    there = columns.at[on * 2 + 1 - zh]
    second_far = net.push(there, there, x=3)
    own.wait()
    for copy in (first_down, first_far, second_up, second_far):
        copy.wait_recv()

    def wanted(k, core):
        found, source = block_at(owner, x * 4 + zh * 2 + core, (y + k) % 4)
        valid = (found == 1) & (source % 2 == c)
        return columns[jnp.where(valid, source // 2, 0)] * jnp.where(valid, 1.0, 0.0)

    swapped = {}
    for k in (2, 1, 3, 0):
        leave[k] = wanted(k, 1 - c)
        swapped[k] = net.push(leave.at[k], enter.at[k], c=1)
    sent = {}
    for k in (2, 1, 3, 0):
        ready[k] = wanted(k, c)
        swapped[k].wait_recv()
        ready[k] = ready[k] + enter[k]
        if k:
            sent[k] = net.push(ready.at[k], parts.at[:, y], y=k)
        else:
            own = net.move(ready.at[0], parts.at[:, y])

    own_piece.wait()
    for copy in (y_down, y_far, other_up, other_far):
        copy.wait_recv()
    for h in range(2):
        for n in range(5):
            i, j = PACKED[h][n]
            stat[pl.ds(i * 256, 256), pl.ds(j * 256, 256)] = sall[h, n].reshape(256, 256)
    for i, j in ((0, 1), (0, 2), (0, 3), (2, 1), (3, 1), (2, 3)):
        stat[pl.ds(j * 256, 256), pl.ds(i * 256, 256)] = stat[pl.ds(i * 256, 256), pl.ds(j * 256, 256)].T
    find_root((y, zl), stat, rootbuf, column, base, high, low)
    returned = net.push(rootbuf.at[1], roots.at[side], side=1)
    kept = net.move(rootbuf.at[0], roots.at[side])

    own.wait()
    halves = []
    for k in (0, 1, 3, 2):
        if k:
            sent[k].wait_recv()
        at = (y + 4 - k) % 4
        halves.append(net.push(parts.at[pl.ds(3, 2), at], crossed.at[:, at], half=1))
    for copy in halves:
        copy.wait_recv()
    kept.wait()
    returned.wait_recv()
    net.close()


def finish_kernel(spot, packed, crossed, old, new):
    half, present = spot[0], spot[1]

    @pl.when(present == 0)
    def _():
        new[...] = 0.6 * old[...]

    @pl.when(present != 0)
    def _():
        def put(i, j, values):
            new[pl.ds(i * 256, 256), pl.ds(j * 256, 256)] = values

        @pl.when(half == 0)
        def _():
            put(0, 0, packed[0])
            put(0, 1, packed[1])
            put(0, 2, packed[3])
            put(0, 3, packed[4])
            put(1, 0, packed[1].T)
            put(1, 1, packed[2])
            put(1, 2, crossed[0].T)
            put(1, 3, crossed[1].T)

        @pl.when(half == 1)
        def _():
            put(0, 0, crossed[0].T)
            put(0, 1, packed[3])
            put(0, 2, packed[0])
            put(0, 3, packed[1])
            put(1, 0, crossed[1].T)
            put(1, 1, packed[4])
            put(1, 2, packed[1].T)
            put(1, 3, packed[2])


def local_call(kernel, out_shape, operands, scratch, flops, traffic):
    return pl.pallas_call(
        kernel,
        out_shape=out_shape,
        in_specs=[pl.BlockSpec(memory_space=pltpu.SMEM)]
        + [pl.BlockSpec(memory_space=pltpu.VMEM)] * (len(operands) - 1),
        out_specs=jax.tree.map(lambda _: pl.BlockSpec(memory_space=pltpu.VMEM), out_shape),
        scratch_shapes=scratch,
        cost_estimate=pl.CostEstimate(flops=flops, bytes_accessed=traffic, transcendentals=0),
        compiler_params=pltpu.CompilerParams(vmem_limit_bytes=VMEM_LIMIT),
    )(*operands)


def f32(*shape):
    return jax.ShapeDtypeStruct(shape, jnp.float32)


def refresh(owner, grads, old):
    strips = (GROUPS, 4, SUB, BS)
    piece = (5, 64, 256)
    scratch = [strips, strips, strips, (2, 64, BS), (2, 64, BS), (4, 64, BS), strips, strips, (GROUPS, 3, SUB, BS)]
    scratch += [(5, 256, 256), (4, *piece), (16, 5, 16, 256), (8, 5, 16, 256), (8, 5, 16, 256), (8, 5, 16, 256)]
    scratch += [(4, 5, 16, 256), (4, 5, 16, 256), piece]
    scratch += [(2, GROUPS, 4, SUB, 256), (4, 4, 64, 256), (5, 256, 256), (3, *piece), (2, 5, 4, 64, 256)]
    scratch += [(BS, BS), (BS, 1), (BS, BS), (2, 64, BS)]
    scratch += [(8, *piece), (4, *piece), (4, *piece), (4, *piece), piece]
    halves = [(4, 256, 256), (4, 256, 256), (BS, BS), (BS, BS)]
    out_shape = (f32(5, 4, 64, 256), f32(2, 4, 64, 256), f32(2, 64, BS))
    return pl.pallas_call(
        refresh_kernel,
        out_shape=out_shape,
        in_specs=[pl.BlockSpec(memory_space=pltpu.SMEM)] + [pl.BlockSpec(memory_space=pl.ANY)] * 2,
        out_specs=tuple(pl.BlockSpec(memory_space=pl.ANY) for _ in out_shape),
        scratch_shapes=[pltpu.VMEM(shape, jnp.float32) for shape in scratch]
        + [pltpu.VMEM(shape, jnp.bfloat16) for shape in halves]
        + [
            pltpu.SemaphoreType.DMA((80,)),
            pltpu.SemaphoreType.DMA((80,)),
            pltpu.SemaphoreType.DMA((24,)),
        ],
        compiler_params=pltpu.CompilerParams(
            collective_id=0, has_side_effects=True, vmem_limit_bytes=VMEM_LIMIT
        ),
    )(owner, grads, old)


def per_device(grads, owner, stats):
    block = lax.axis_index("block")
    y, zl, *_ = place(lax.axis_index("dp"), block)
    old = stats[0, 0]
    parts, crossed, roots = refresh(owner, grads.reshape(4, 4, 64, BS), old)
    present = jnp.sum((owner == block).astype(jnp.int32)) > y
    new = local_call(
        finish_kernel,
        f32(512, BS),
        [
            jnp.stack([zl % 2, present.astype(jnp.int32)]).astype(jnp.int32),
            parts.reshape(5, 256, 256),
            crossed.reshape(2, 256, 256),
            old,
        ],
        [],
        2**20,
        6 * 2**20,
    )
    return new[None, None], roots[None]


def solution(mesh):
    return jax.shard_map(
        per_device,
        mesh=mesh,
        in_specs=(P("dp", "block", None, None), P(), P("block", "dp", None, None)),
        out_specs=(P("block", "dp", None, None), P("block", None, "dp", None)),
        check_vma=False,
    )
```

```python
import jax
import jax.numpy as jnp
from jax import lax
from jax.experimental import pallas as pl
from jax.experimental.pallas import tpu as pltpu
from jax.sharding import PartitionSpec as P

PSTEPS = 8
BS = 1024
GROUPS = 4
SUB = 64 // GROUPS
MESH = pl.DeviceIdType.MESH
VMEM_LIMIT = 60 * 1024 * 1024

PACKED = (
    ((0, 2), (0, 3), (0, 0), (0, 1), (1, 1)),
    ((2, 1), (3, 1), (2, 2), (2, 3), (3, 3)),
)
SETS = (pl.ds(0, 2), pl.ds(2, 3))


GRADS, OLD = 0, 1
ORDER = (
    (GRADS, 1, 0), (GRADS, 0, 2), (OLD, 2, 0), (GRADS, 1, 1), (GRADS, 2, 0), (OLD, 1, 1), (GRADS, 0, 3),
    (GRADS, 1, 2), (GRADS, 3, 0), (GRADS, 2, 1), (GRADS, 4, 0), (OLD, 3, 0), (GRADS, 1, 3), (GRADS, 3, 1),
    (GRADS, 2, 2), (GRADS, 5, 0), (GRADS, 4, 1), (OLD, 4, 0), (OLD, 2, 1), (GRADS, 2, 3), (GRADS, 3, 2),
    (GRADS, 6, 0), (GRADS, 5, 1), (GRADS, 4, 2), (OLD, 5, 0), (OLD, 3, 1), (GRADS, 3, 3), (GRADS, 6, 1),
    (GRADS, 5, 2), (GRADS, 4, 3), (OLD, 4, 1), (GRADS, 6, 2), (GRADS, 5, 3), (GRADS, 6, 3), (OLD, 5, 1),
)


def place(dp, block):
    return dp // 4, dp % 4, block // 4, block // 2 % 2, block % 2


class Network:
    def __init__(self, send, recv, local):
        self.send, self.recv, self.local = send, recv, local
        self.count = self.locals = 0
        self.sent = []
        self.dp, self.block = lax.axis_index("dp"), lax.axis_index("block")
        self.y, self.zl, self.x, self.zh, self.c = place(self.dp, self.block)

    def device(self, y=0, zl=0, x=0, zh=0, c=0, half=0, side=0):
        row = (self.zl + zl) % 4
        if half:
            row = row + 1 - 2 * (row % 2)
        if side:
            row = (row + 2) % 4
        return (
            (self.y + y) % 4 * 4 + row,
            (self.x + x) % 4 * 4 + (self.zh + zh) % 2 * 2 + (self.c + c) % 2,
        )

    def greet(self, steps):
        barrier = pltpu.get_barrier_semaphore()
        for step in steps:
            pl.semaphore_signal(barrier, inc=1, device_id=self.device(**step), device_id_type=MESH)
        pl.semaphore_wait(barrier, len(steps))

    def push(self, source, target, **step):
        n = self.count
        self.count += 1
        copy = pltpu.make_async_remote_copy(
            src_ref=source,
            dst_ref=target,
            send_sem=self.send.at[n],
            recv_sem=self.recv.at[n],
            device_id=self.device(**step),
            device_id_type=MESH,
        )
        copy.start()
        self.sent.append(copy)
        return copy

    def move(self, source, target):
        copy = pltpu.make_async_copy(source, target, self.local.at[self.locals])
        self.locals += 1
        copy.start()
        return copy

    def close(self):
        for copy in self.sent:
            copy.wait_send()


def split(values):
    high = values.astype(jnp.bfloat16)
    return high, (values - high.astype(jnp.float32)).astype(jnp.bfloat16)


def rank_of(owner, block):
    mine = owner[block]
    count = lax.fori_loop(
        0, 16, lambda i, n: n + jnp.where((i < block) & (owner[i] == mine), 1, 0), jnp.int32(0)
    )
    return mine, count


def block_at(owner, column, wanted):
    def step(i, carry):
        count, found, source = carry
        hit = owner[i] == column
        here = hit & (count == wanted)
        return count + jnp.where(hit, 1, 0), jnp.where(here, 1, found), jnp.where(here, i, source)

    zero = jnp.int32(0)
    _, found, source = lax.fori_loop(0, 16, step, (zero, zero, zero))
    return found, source


def top_value(stat, column):

    def to_column(row):
        @pl.loop(0, 8)
        def _(i):
            rows = pl.ds(pl.multiple_of(i * 128, 128), 128)
            column[rows, :] = jnp.sum(stat[rows, :] * row, axis=1, keepdims=True)

        return column[...]

    def to_row(values):
        column[...] = values

        def body(i, total):
            rows = pl.ds(pl.multiple_of(i * 128, 128), 128)
            return total + jnp.sum(stat[rows, :] * column[rows, :], axis=0, keepdims=True)

        return lax.fori_loop(0, 8, body, jnp.zeros((1, BS), jnp.float32))

    row = jnp.full((1, BS), BS ** (-0.5), jnp.float32)
    for _ in range(PSTEPS // 2):
        image = to_column(row)
        image = image / jnp.sqrt(jnp.sum(image * image))
        row = to_row(image)
        row = row / jnp.sqrt(jnp.sum(row * row))
    image = to_column(row)
    return jnp.sqrt(jnp.sum(image * image, axis=(0, 1), keepdims=True))


def find_root(spot, top, stat, root, base, high, low):
    y, zl = spot
    scale = 2.5 / top
    fourth = jnp.sqrt(jnp.sqrt(scale))

    @pl.loop(0, 4)
    def _(i):
        rows = pl.ds(pl.multiple_of(i * 256, 256), 256)
        eye = lax.broadcasted_iota(jnp.int32, (256, BS), 0) + i * 256 == lax.broadcasted_iota(
            jnp.int32, (256, BS), 1
        )
        values = (jnp.where(eye, 5.0, 0.0) - scale * stat[rows, :]) / 4.0
        base[rows, :] = values
        upper, lower = split(values)
        high[rows, :] = upper
        low[rows, :] = lower

    def times(left):
        upper, lower = split(left)

        def product(a, b):
            return jnp.dot(a, b, preferred_element_type=jnp.float32)

        both = product(jnp.concatenate([upper, lower], axis=0), high[...])
        return both[128:] + product(upper, low[...]) + both[:128]

    own = pl.multiple_of((y * 4 + zl) * 64, 64)
    other = pl.multiple_of((y * 4 + (zl + 2) % 4) * 64, 64)
    first = jnp.concatenate([base[pl.ds(own, 64), :], base[pl.ds(other, 64), :]], axis=0)
    power = times(times(times(first)))
    result = (5.0 * first + times(4.0 * times(power) - 5.0 * power)) * (fourth / 4.0)
    root[0] = result[:64]
    root[1] = result[64:]


def refresh_kernel(owner, grads, old, new_out, roots, *scratch):
    far, up, down, stage, mine, middle, first_got, second_got, toward, away, home = scratch[:11]
    packed, slots, oldp, both, chunk, gram, ggot, sall, stat, column, base, rootbuf = scratch[11:23]
    piece, parts, crossed, new = scratch[23:27]
    spread, outgo, income, near, cross, fin = (scratch[27 + 2 * n : 29 + 2 * n] for n in range(6))
    columns, leave, enter, ready = (scratch[39 + 2 * n : 41 + 2 * n] for n in range(4))
    mat_high, mat_low, high, low = scratch[47:51]
    net = Network(*scratch[51:])
    y, zl, x, zh, c = net.y, net.zl, net.x, net.zh, net.c
    side, half = zl // 2, zl % 2
    below, above, beyond = (y + 3) % 4, (y + 1) % 4, (y + 2) % 4

    def rows_of(at, size):
        return pl.ds(pl.multiple_of(at * size, size), size)

    def strip(ref, chunk_at, first, group):
        return ref.at[chunk_at, pl.ds(first, 2), pl.ds(group * SUB, SUB)]

    fetched = []
    for n in range(5):
        i = jnp.where(half == 0, PACKED[0][n][0], PACKED[1][n][0] - 2)
        j = jnp.where(half == 0, PACKED[0][n][1], PACKED[1][n][1])
        fetched.append(net.move(old.at[rows_of(i, 256), rows_of(j, 256)], packed.at[n]))
    prefetch = [
        net.move(grads.at[above, pl.ds(0, 2)], toward),
        net.move(grads.at[below, pl.ds(2, 2)], away),
        net.move(grads.at[y], home),
    ]
    kept_old = net.move(old, new)
    net.greet(
        [dict(y=1), dict(y=2), dict(y=3), dict(half=1), dict(side=1)]
        + [dict(x=1), dict(x=2), dict(x=3), dict(zh=1), dict(c=1)]
    )

    def scatter(group):
        far_up = net.push(strip(grads, beyond, 0, group), far.at[group, pl.ds(0, 2)], y=1)
        far_down = net.push(strip(grads, beyond, 2, group), far.at[group, pl.ds(2, 2)], y=3)
        near_up = net.push(strip(grads, above, 2, group), up.at[group, pl.ds(2, 2)], y=1)
        near_down = net.push(strip(grads, below, 0, group), down.at[group, pl.ds(0, 2)], y=3)
        return far_up, far_down, near_up, near_down

    def relay(group, copies):
        rows = pl.ds(group * SUB, SUB)
        copies[0].wait_recv()
        stage[group, 0:2] = far[group, 0:2] + toward[:, rows]
        first = net.push(stage.at[group, pl.ds(0, 2)], up.at[group, pl.ds(0, 2)], y=1)
        copies[1].wait_recv()
        stage[group, 2:4] = far[group, 2:4] + away[:, rows]
        second = net.push(stage.at[group, pl.ds(2, 2)], down.at[group, pl.ds(2, 2)], y=3)
        return first, second, copies[2], copies[3]

    def reduce_half(group, copies):
        for copy in copies:
            copy.wait_recv()
        for n in range(4):
            mine[group, n % 2, n // 2] = home[n, pl.ds(group * SUB, SUB)] + up[group, n] + down[group, n]
        return net.push(mine.at[group, 1 - half], first_got.at[group], half=1)

    def reduce_side(group, copy):
        copy.wait_recv()
        middle[group] = mine[group, half] + first_got[group]
        return net.push(middle.at[group, 1 - side], second_got.at[group], side=1)

    def turn(group, copy):
        copy.wait_recv()
        total = middle[group, side] + second_got[group]
        for a in range(4):
            both[1, group, a] = total[:, a * 256 : (a + 1) * 256]
        kept = net.move(both.at[1, group, y], both.at[0, group, y])
        return [net.push(both.at[1, group, (y + k) % 4], both.at[0, group, y], y=k) for k in (1, 3, 2)], kept

    def rows_in(device, group):
        return chunk.at[:, device, pl.ds(group * SUB, SUB)]

    def gather_side(group, turned):
        copies, kept = turned
        for copy in copies:
            copy.wait_recv()
        kept.wait()
        here = rows_in(zl, group)
        from_side = net.push(both.at[1 - side, group], here, side=1)
        from_half = net.push(both.at[side, group], here, half=1)
        return from_side, from_half, net.move(both.at[side, group], here)

    def gather_half(group, copies):
        copies[0].wait_recv()
        there = rows_in((zl + 2) % 4, group)
        return net.push(there, there, half=1), copies[1], copies[2]

    def start_old(n):
        part = SETS[n]
        own = net.move(packed.at[part, rows_of(y, 64)], slots.at[y, part])
        return own, {
            k: net.push(packed.at[part, rows_of((y + k) % 4, 64)], slots.at[y, part], y=k) for k in (1, 3, 2)
        }

    def spread_old(n, started):
        own, slotted = started
        local, remote = [], []
        for k in (0, 1, 3, 2):
            if k == 0:
                own.wait()
            else:
                slotted[k].wait_recv()
            at = (y + 4 - k) % 4
            for m in (0, 1, 2, 3):
                source = slots.at[at, SETS[n], rows_of((x + m) % 4, 16)]
                if m == 0:
                    local.append(net.move(source, spread[n].at[x * 4 + at]))
                else:
                    remote.append(net.push(source, spread[n].at[x * 4 + at], x=m))
        return local, remote

    def swap_old(n, spreads):
        for copy in spreads[0]:
            copy.wait()
        for copy in spreads[1]:
            copy.wait_recv()
        for i, (index, mask) in enumerate(old_away):
            outgo[n][i] = spread[n][index] * mask
        return net.push(outgo[n], income[n], c=1)

    def cross_old(n, swapped):
        for i, (index, mask) in enumerate(old_home):
            near[n][i] = spread[n][index] * mask
        swapped.wait_recv()
        for i in range(8):
            near[n][i] = near[n][i] + income[n][i]
        return net.push(near[n].at[pl.ds(4, 4)], cross[n], zh=1)

    def finish_old(n, crossing):
        crossing.wait_recv()
        for i in range(4):
            fin[n][i] = near[n][i] + cross[n][i]
        here = oldp.at[SETS[n], rows_of(x, 16)]
        own = net.move(fin[n].at[0], here)
        return own, [net.push(fin[n].at[m], here, x=m) for m in (1, 2, 3)]

    def lookup_old(n, core):
        target = (x + n % 4) % 4 * 4 + (zh + n // 4) % 2 * 2 + core
        source, slot = rank_of(owner, target)
        valid = (source // 2 % 2 == zh) & (source % 2 == c)
        return jnp.where(valid, source // 4 * 4 + slot, 0), jnp.where(valid, 1.0, 0.0)

    def lookup_slot(k, core):
        found, source = block_at(owner, x * 4 + zh * 2 + core, (y + k) % 4)
        valid = (found == 1) & (source % 2 == c)
        return jnp.where(valid, source // 2, 0), jnp.where(valid, 1.0, 0.0)

    stages = (scatter, relay, reduce_half, reduce_side, turn, gather_side, gather_half)
    steps = (None, start_old, spread_old, swap_old, cross_old, finish_old)
    state, olds = {}, {}

    def run(stage, group):
        if stage == 0:
            state[group] = scatter(group)
        else:
            state[group] = stages[stage](group, state[group])

    def run_old(step, n):
        if step == 1:
            olds[n] = start_old(n)
        else:
            olds[n] = steps[step](n, olds[n])

    run(0, 0)
    for copy in fetched:
        copy.wait()
    run_old(1, 0)
    run(0, 1)
    old_away = [lookup_old(n, 1 - c) for n in range(8)]
    old_home = [lookup_old(n, c) for n in range(8)]
    for copy in prefetch:
        copy.wait()
    for job in ORDER:
        if job[0] == GRADS:
            run(job[1], job[2])
        else:
            run_old(job[1], job[2])
    kept_old.wait()
    members = lax.fori_loop(0, 16, lambda i, n: n + jnp.where(owner[i] == net.block, 1, 0), jnp.int32(0))
    new[...] = new[...] * jnp.where(members > y, 0.0, 0.6)
    slot_away = [lookup_slot(k, 1 - c) for k in range(4)]
    slot_home = [lookup_slot(k, c) for k in range(4)]
    for relayed, direct, kept in state.values():
        relayed.wait_recv()
        direct.wait_recv()
        kept.wait()

    @pl.when(side == 1)
    def _():
        for a in range(4):
            mat_high[a], mat_low[a] = split(chunk[a].reshape(256, 256).T)

    @pl.when(side == 0)
    def _():
        for a in range(4):
            mat_high[a], mat_low[a] = split(chunk[a].reshape(256, 256))

    def outer(a, b):
        return lax.dot_general(a, b, (((1,), (1,)), ((), ())), preferred_element_type=jnp.float32)

    summed = []
    for part in SETS:
        for n in range(part.start, part.start + part.size):
            i = jnp.where(half == 0, PACKED[0][n][0], PACKED[1][n][0])
            j = jnp.where(half == 0, PACKED[0][n][1], PACKED[1][n][1])
            left_high, right_high = mat_high[i], mat_high[j]
            gram[n] = (
                outer(left_high, mat_low[j]) + outer(mat_low[i], right_high) + outer(left_high, right_high)
            )
        summed.append(
            [
                net.push(gram.at[part, rows_of((y + k) % 4, 64)], ggot.at[k - 1, part], y=k)
                for k in (1, 3, 2)
            ]
        )
    back, on = (x + 3) % 4, (x + 1) % 4
    own, across, first_up, first_down = [], [], [], []
    halved, y_up, y_down, y_far, other_up, other_down, other_far, own_piece = [], [], [], [], [], [], [], []
    for n, part in enumerate(SETS):
        olds[n][0].wait()
        for copy in olds[n][1]:
            copy.wait_recv()
        for copy in summed[n]:
            copy.wait_recv()
        piece[part] = 0.6 * oldp[part] + (1.0 - 0.6) * (
            gram[part, rows_of(y, 64)] + ggot[0, part] + ggot[1, part] + ggot[2, part]
        )
        here, there = columns[n].at[x * 2 + zh], sall.at[half, part, y]
        halved.append(net.push(piece.at[part], there, half=1))
        across.append(net.push(piece.at[part], here, zh=1))
        first_up.append(net.push(piece.at[part], here, x=1))
        first_down.append(net.push(piece.at[part], here, x=3))
        y_up.append(net.push(piece.at[part], there, y=1))
        y_down.append(net.push(piece.at[part], there, y=3))
        own.append(net.move(piece.at[part], here))
        own_piece.append(net.move(piece.at[part], there))

    first_far, second_up, second_down, second_far = [], [], [], []

    def pass_first(n):
        first_up[n].wait_recv()
        there = columns[n].at[back * 2 + zh]
        first_far.append(net.push(there, there, x=1))

    def start_second(n):
        across[n].wait_recv()
        there = columns[n].at[x * 2 + 1 - zh]
        second_down.append(net.push(there, there, x=3))
        second_up.append(net.push(there, there, x=1))

    def pass_second(n):
        second_down[n].wait_recv()
        there = columns[n].at[on * 2 + 1 - zh]
        second_far.append(net.push(there, there, x=3))

    def choose(n):
        own[n].wait()
        for copy in (first_down[n], first_far[n], second_up[n], second_far[n]):
            copy.wait_recv()
        swapped = {}
        for k in (2, 1, 3, 0):
            index, mask = slot_away[k]
            leave[n][k] = columns[n][index] * mask
            swapped[k] = net.push(leave[n].at[k], enter[n].at[k], c=1)
        sent = {}
        for k in (2, 1, 3, 0):
            index, mask = slot_home[k]
            ready[n][k] = columns[n][index] * mask
            swapped[k].wait_recv()
            ready[n][k] = ready[n][k] + enter[n][k]
            here = parts.at[SETS[n], y]
            if k:
                sent[k] = net.push(ready[n].at[k], here, y=k)
            else:
                kept = net.move(ready[n].at[0], here)
        return sent, kept

    def pass_own(n):
        y_up[n].wait_recv()
        there = sall.at[half, SETS[n], below]
        y_far.append(net.push(there, there, y=1))

    def start_other(n):
        halved[n].wait_recv()
        there = sall.at[1 - half, SETS[n], y]
        other_down.append(net.push(there, there, y=3))
        other_up.append(net.push(there, there, y=1))

    def pass_other(n):
        other_down[n].wait_recv()
        there = sall.at[1 - half, SETS[n], above]
        other_far.append(net.push(there, there, y=3))

    pass_first(0)
    pass_own(0)
    start_other(0)
    start_second(0)
    pass_first(1)
    pass_own(1)
    start_other(1)
    pass_second(0)
    pass_other(0)
    start_second(1)
    pass_other(1)
    sent = [choose(0)]
    pass_second(1)

    for n in range(2):
        own_piece[n].wait()
        for copy in (y_down[n], y_far[n], other_up[n], other_far[n]):
            copy.wait_recv()
    for h in range(2):
        for n in range(5):
            i, j = PACKED[h][n]
            stat[pl.ds(i * 256, 256), pl.ds(j * 256, 256)] = sall[h, n].reshape(256, 256)
    for i, j in ((0, 1), (0, 2), (0, 3), (2, 1), (3, 1), (2, 3)):
        stat[pl.ds(j * 256, 256), pl.ds(i * 256, 256)] = stat[pl.ds(i * 256, 256), pl.ds(j * 256, 256)].T
    top = top_value(stat, column)
    sent.append(choose(1))

    halves = []
    for k in (0, 1, 3, 2):
        if k:
            sent[0][0][k].wait_recv()
        else:
            sent[0][1].wait()
        at = (y + 4 - k) % 4
        halves.append(net.push(parts.at[SETS[0], at], crossed.at[:, at], half=1))
    find_root((y, zl), top, stat, rootbuf, base, high, low)
    returned = net.push(rootbuf.at[1], roots.at[side], side=1)
    kept = net.move(rootbuf.at[0], roots.at[side])

    sent[1][1].wait()
    for k in (1, 3, 2):
        sent[1][0][k].wait_recv()
    for copy in halves:
        copy.wait_recv()

    def put(i, j, values):
        rows, cols = pl.ds(i * 256, 256), pl.ds(j * 256, 256)
        new[rows, cols] = new[rows, cols] + values

    def part(n):
        return parts[n].reshape(256, 256)

    def turned_part(n):
        return crossed[n].reshape(256, 256).T

    @pl.when(half == 0)
    def _():
        put(0, 0, part(2))
        put(0, 1, part(3))
        put(0, 2, part(0))
        put(0, 3, part(1))
        put(1, 0, part(3).T)
        put(1, 1, part(4))
        put(1, 2, turned_part(0))
        put(1, 3, turned_part(1))

    @pl.when(half == 1)
    def _():
        put(0, 0, turned_part(0))
        put(0, 1, part(0))
        put(0, 2, part(2))
        put(0, 3, part(3))
        put(1, 0, turned_part(1))
        put(1, 1, part(1))
        put(1, 2, part(3).T)
        put(1, 3, part(4))

    written = net.move(new, new_out)
    kept.wait()
    returned.wait_recv()
    written.wait()
    net.close()


def f32(*shape):
    return jax.ShapeDtypeStruct(shape, jnp.float32)


def refresh(owner, grads, old):
    strips, rows = (GROUPS, 4, SUB, BS), (GROUPS, 2, SUB, BS)
    piece = (5, 64, 256)
    scratch = [strips, strips, strips, strips, (GROUPS, 2, 2, SUB, BS), rows, rows, (GROUPS, SUB, BS)]
    scratch += [(2, 64, BS), (2, 64, BS), (4, 64, BS), (5, 256, 256), (4, *piece), piece]
    scratch += [(2, GROUPS, 4, SUB, 256), (4, 4, 64, 256), (5, 256, 256), (3, *piece), (2, 5, 4, 64, 256)]
    scratch += [(BS, BS), (BS, 1), (BS, BS), (2, 64, BS)]
    scratch += [piece, (5, 4, 64, 256), (2, 4, 64, 256), (512, BS)]
    for count, rows in ((16, 16), (8, 16), (8, 16), (8, 16), (4, 16), (4, 16), (8, 64), (4, 64), (4, 64), (4, 64)):
        scratch += [(count, part.size, rows, 256) for part in SETS]
    halves = [(4, 256, 256), (4, 256, 256), (BS, BS), (BS, BS)]
    out_shape = (f32(512, BS), f32(2, 64, BS))
    return pl.pallas_call(
        refresh_kernel,
        out_shape=out_shape,
        in_specs=[pl.BlockSpec(memory_space=pltpu.SMEM)] + [pl.BlockSpec(memory_space=pl.ANY)] * 2,
        out_specs=tuple(pl.BlockSpec(memory_space=pl.ANY) for _ in out_shape),
        scratch_shapes=[pltpu.VMEM(shape, jnp.float32) for shape in scratch]
        + [pltpu.VMEM(shape, jnp.bfloat16) for shape in halves]
        + [
            pltpu.SemaphoreType.DMA((160,)),
            pltpu.SemaphoreType.DMA((160,)),
            pltpu.SemaphoreType.DMA((48,)),
        ],
        compiler_params=pltpu.CompilerParams(
            collective_id=0, has_side_effects=True, vmem_limit_bytes=VMEM_LIMIT
        ),
    )(owner, grads, old)


def per_device(grads, owner, stats):
    new, roots = refresh(owner, grads.reshape(4, 4, 64, BS), stats[0, 0])
    return new[None, None], roots[None]


def solution(mesh):
    return jax.shard_map(
        per_device,
        mesh=mesh,
        in_specs=(P("dp", "block", None, None), P(), P("block", "dp", None, None)),
        out_specs=(P("block", "dp", None, None), P("block", None, "dp", None)),
        check_vma=False,
    )
```

```python
import jax
import jax.numpy as jnp
from jax import lax
from jax.experimental import pallas as pl
from jax.experimental.pallas import tpu as pltpu
from jax.sharding import PartitionSpec as P

PSTEPS = 8
BS = 1024
GROUPS = 4
SUB = 64 // GROUPS
MESH = pl.DeviceIdType.MESH
VMEM_LIMIT = 60 * 1024 * 1024

PACKED = (
    ((0, 2), (0, 3), (0, 0), (0, 1), (1, 1)),
    ((2, 1), (3, 1), (2, 2), (2, 3), (3, 3)),
)
OLD_SETS = (pl.ds(0, 2), pl.ds(2, 3))
SETS = (pl.ds(0, 2), pl.ds(2, 2), pl.ds(4, 1))


GRADS, OLD = 0, 1
ORDER = (
    (GRADS, 2, 0), (GRADS, 1, 1), (GRADS, 0, 2), (GRADS, 2, 1), (GRADS, 3, 0), (GRADS, 1, 2), (GRADS, 0, 3),
    (GRADS, 2, 2), (GRADS, 4, 0), (GRADS, 3, 1), (GRADS, 1, 3), (OLD, 2, 0), (GRADS, 2, 3), (GRADS, 5, 0),
    (GRADS, 4, 1), (GRADS, 3, 2), (OLD, 1, 1), (GRADS, 6, 0), (GRADS, 5, 1), (GRADS, 4, 2), (GRADS, 3, 3),
    (OLD, 3, 0), (GRADS, 7, 0), (GRADS, 6, 1), (GRADS, 5, 2), (GRADS, 4, 3), (OLD, 4, 0), (OLD, 2, 1), (GRADS, 7, 1),
    (GRADS, 6, 2), (GRADS, 5, 3), (OLD, 3, 1), (GRADS, 7, 2), (GRADS, 6, 3), (OLD, 5, 0), (OLD, 4, 1), (GRADS, 7, 3),
    (OLD, 5, 1),
)


def place(dp, block):
    return dp // 4, dp % 4, block // 4, block // 2 % 2, block % 2


class Network:
    def __init__(self, send, recv, local):
        self.send, self.recv, self.local = send, recv, local
        self.count = self.locals = 0
        self.sent = []
        self.dp, self.block = lax.axis_index("dp"), lax.axis_index("block")
        self.y, self.zl, self.x, self.zh, self.c = place(self.dp, self.block)

    def device(self, y=0, zl=0, x=0, zh=0, c=0, half=0, side=0):
        row = (self.zl + zl) % 4
        if half:
            row = row + 1 - 2 * (row % 2)
        if side:
            row = (row + 2) % 4
        return (
            (self.y + y) % 4 * 4 + row,
            (self.x + x) % 4 * 4 + (self.zh + zh) % 2 * 2 + (self.c + c) % 2,
        )

    def greet(self, steps):
        barrier = pltpu.get_barrier_semaphore()
        for step in steps:
            pl.semaphore_signal(barrier, inc=1, device_id=self.device(**step), device_id_type=MESH)
        pl.semaphore_wait(barrier, len(steps))

    def push(self, source, target, **step):
        n = self.count
        self.count += 1
        copy = pltpu.make_async_remote_copy(
            src_ref=source,
            dst_ref=target,
            send_sem=self.send.at[n],
            recv_sem=self.recv.at[n],
            device_id=self.device(**step),
            device_id_type=MESH,
        )
        copy.start()
        self.sent.append(copy)
        return copy

    def move(self, source, target):
        copy = pltpu.make_async_copy(source, target, self.local.at[self.locals])
        self.locals += 1
        copy.start()
        return copy

    def close(self):
        for copy in self.sent:
            copy.wait_send()


def split(values):
    high = values.astype(jnp.bfloat16)
    return high, (values - high.astype(jnp.float32)).astype(jnp.bfloat16)


def rank_of(owner, block):
    mine = owner[block]
    count = lax.fori_loop(
        0, 16, lambda i, n: n + jnp.where((i < block) & (owner[i] == mine), 1, 0), jnp.int32(0)
    )
    return mine, count


def block_at(owner, column, wanted):
    def step(i, carry):
        count, found, source = carry
        hit = owner[i] == column
        here = hit & (count == wanted)
        return count + jnp.where(hit, 1, 0), jnp.where(here, 1, found), jnp.where(here, i, source)

    zero = jnp.int32(0)
    _, found, source = lax.fori_loop(0, 16, step, (zero, zero, zero))
    return found, source


def top_value(stat, column):

    def to_column(row):
        for i in range(8):
            rows = pl.ds(i * 128, 128)
            column[rows, :] = jnp.sum(stat[rows, :] * row, axis=1, keepdims=True)
        return column[...]

    def to_row(values):
        column[...] = values
        total = jnp.zeros((8, BS), jnp.float32)
        for i in range(8):
            rows = pl.ds(i * 128, 128)
            total = total + jnp.sum((stat[rows, :] * column[rows, :]).reshape(16, 8, BS), axis=0)
        return jnp.sum(total, axis=0, keepdims=True)

    def norm(values):
        return jnp.sqrt(jnp.sum(values * values, axis=(0, 1), keepdims=True))

    row = jnp.full((1, BS), BS ** (-0.5), jnp.float32)
    for _ in range(PSTEPS // 2):
        image = to_column(row)
        row = to_row(image * (1.0 / norm(image)))
        row = row * (1.0 / norm(row))
    return norm(to_column(row))


def find_root(spot, top, stat, root, base, high, low):
    y, zl = spot
    scale = 2.5 / top
    fourth = jnp.sqrt(jnp.sqrt(scale))

    @pl.loop(0, 4)
    def _(i):
        rows = pl.ds(pl.multiple_of(i * 256, 256), 256)
        eye = lax.broadcasted_iota(jnp.int32, (256, BS), 0) + i * 256 == lax.broadcasted_iota(
            jnp.int32, (256, BS), 1
        )
        values = (jnp.where(eye, 5.0, 0.0) - scale * stat[rows, :]) / 4.0
        base[rows, :] = values
        upper, lower = split(values)
        high[rows, :] = upper
        low[rows, :] = lower

    def times(left):
        upper, lower = split(left)

        def product(a, b):
            return jnp.dot(a, b, preferred_element_type=jnp.float32)

        both = product(jnp.concatenate([upper, lower], axis=0), high[...])
        return both[128:] + product(upper, low[...]) + both[:128]

    own = pl.multiple_of((y * 4 + zl) * 64, 64)
    other = pl.multiple_of((y * 4 + (zl + 2) % 4) * 64, 64)
    first = jnp.concatenate([base[pl.ds(own, 64), :], base[pl.ds(other, 64), :]], axis=0)
    power = times(times(times(first)))
    result = (5.0 * first + times(4.0 * times(power) - 5.0 * power)) * (fourth / 4.0)
    root[0] = result[:64]
    root[1] = result[64:]


def refresh_kernel(owner, grads, old, new_out, roots, *scratch):
    far, up, down, stage, mine, middle, first_got, second_got, toward, away, home = scratch[:11]
    packed, slots, oldp, both, chunk, gram, ggot, sall, stat, column, base, rootbuf = scratch[11:23]
    piece, parts, crossed, new = scratch[23:27]
    spread, outgo, income, near, cross, fin = (scratch[27 + 2 * n : 29 + 2 * n] for n in range(6))
    columns, leave, enter, ready = (scratch[39 + 3 * n : 42 + 3 * n] for n in range(4))
    mat_high, mat_low, high, low = scratch[51:55]
    net = Network(*scratch[55:])
    y, zl, x, zh, c = net.y, net.zl, net.x, net.zh, net.c
    side, half = zl // 2, zl % 2
    below, above, beyond = (y + 3) % 4, (y + 1) % 4, (y + 2) % 4

    def rows_of(at, size):
        return pl.ds(pl.multiple_of(at * size, size), size)

    def strip(ref, chunk_at, first, group):
        return ref.at[chunk_at, pl.ds(first, 2), pl.ds(group * SUB, SUB)]

    fetched = []
    for n in range(5):
        i = jnp.where(half == 0, PACKED[0][n][0], PACKED[1][n][0] - 2)
        j = jnp.where(half == 0, PACKED[0][n][1], PACKED[1][n][1])
        fetched.append(net.move(old.at[rows_of(i, 256), rows_of(j, 256)], packed.at[n]))
    prefetch = [
        net.move(grads.at[above, pl.ds(0, 2)], toward),
        net.move(grads.at[below, pl.ds(2, 2)], away),
        net.move(grads.at[y], home),
    ]
    kept_old = net.move(old, new)
    net.greet(
        [dict(y=1), dict(y=2), dict(y=3), dict(half=1), dict(side=1)]
        + [dict(x=1), dict(x=2), dict(x=3), dict(zh=1), dict(c=1)]
    )

    def scatter_far(group):
        far_up = net.push(strip(grads, beyond, 0, group), far.at[group, pl.ds(0, 2)], y=1)
        far_down = net.push(strip(grads, beyond, 2, group), far.at[group, pl.ds(2, 2)], y=3)
        return far_up, far_down

    def scatter_near(group, copies):
        near_up = net.push(strip(grads, above, 2, group), up.at[group, pl.ds(2, 2)], y=1)
        near_down = net.push(strip(grads, below, 0, group), down.at[group, pl.ds(0, 2)], y=3)
        return *copies, near_up, near_down

    def relay(group, copies):
        rows = pl.ds(group * SUB, SUB)
        copies[0].wait_recv()
        stage[group, 0:2] = far[group, 0:2] + toward[:, rows]
        first = net.push(stage.at[group, pl.ds(0, 2)], up.at[group, pl.ds(0, 2)], y=1)
        copies[1].wait_recv()
        stage[group, 2:4] = far[group, 2:4] + away[:, rows]
        second = net.push(stage.at[group, pl.ds(2, 2)], down.at[group, pl.ds(2, 2)], y=3)
        return first, second, copies[2], copies[3]

    def reduce_half(group, copies):
        for copy in copies:
            copy.wait_recv()
        for n in range(4):
            mine[group, n % 2, n // 2] = home[n, pl.ds(group * SUB, SUB)] + up[group, n] + down[group, n]
        return net.push(mine.at[group, 1 - half], first_got.at[group], half=1)

    def reduce_side(group, copy):
        copy.wait_recv()
        middle[group] = mine[group, half] + first_got[group]
        return net.push(middle.at[group, 1 - side], second_got.at[group], side=1)

    def turn(group, copy):
        copy.wait_recv()
        total = middle[group, side] + second_got[group]
        for a in range(4):
            both[1, group, a] = total[:, a * 256 : (a + 1) * 256]
        kept = net.move(both.at[1, group, y], both.at[0, group, y])
        return [net.push(both.at[1, group, (y + k) % 4], both.at[0, group, y], y=k) for k in (1, 3, 2)], kept

    def rows_in(device, group):
        return chunk.at[:, device, pl.ds(group * SUB, SUB)]

    def gather_side(group, turned):
        copies, kept = turned
        for copy in copies:
            copy.wait_recv()
        kept.wait()
        here = rows_in(zl, group)
        from_side = net.push(both.at[1 - side, group], here, side=1)
        from_half = net.push(both.at[side, group], here, half=1)
        return from_side, from_half, net.move(both.at[side, group], here)

    def gather_half(group, copies):
        copies[0].wait_recv()
        there = rows_in((zl + 2) % 4, group)
        return net.push(there, there, half=1), copies[1], copies[2]

    def start_old(n):
        part = OLD_SETS[n]
        own = net.move(packed.at[part, rows_of(y, 64)], slots.at[y, part])
        return own, {
            k: net.push(packed.at[part, rows_of((y + k) % 4, 64)], slots.at[y, part], y=k) for k in (1, 3, 2)
        }

    def spread_old(n, started):
        own, slotted = started
        local, remote = [], []
        for k in (0, 1, 3, 2):
            if k == 0:
                own.wait()
            else:
                slotted[k].wait_recv()
            at = (y + 4 - k) % 4
            for m in (0, 1, 2, 3):
                source = slots.at[at, OLD_SETS[n], rows_of((x + m) % 4, 16)]
                if m == 0:
                    local.append(net.move(source, spread[n].at[x * 4 + at]))
                else:
                    remote.append(net.push(source, spread[n].at[x * 4 + at], x=m))
        return local, remote

    def swap_old(n, spreads):
        for copy in spreads[0]:
            copy.wait()
        for copy in spreads[1]:
            copy.wait_recv()
        for i, (index, mask) in enumerate(old_away):
            outgo[n][i] = spread[n][index] * mask
        return net.push(outgo[n], income[n], c=1)

    def cross_old(n, swapped):
        for i, (index, mask) in enumerate(old_home):
            near[n][i] = spread[n][index] * mask
        swapped.wait_recv()
        for i in range(8):
            near[n][i] = near[n][i] + income[n][i]
        return net.push(near[n].at[pl.ds(4, 4)], cross[n], zh=1)

    def finish_old(n, crossing):
        crossing.wait_recv()
        for i in range(4):
            fin[n][i] = near[n][i] + cross[n][i]
        here = oldp.at[OLD_SETS[n], rows_of(x, 16)]
        own = net.move(fin[n].at[0], here)
        return own, [net.push(fin[n].at[m], here, x=m) for m in (1, 2, 3)]

    def lookup_old(n, core):
        target = (x + n % 4) % 4 * 4 + (zh + n // 4) % 2 * 2 + core
        source, slot = rank_of(owner, target)
        valid = (source // 2 % 2 == zh) & (source % 2 == c)
        return jnp.where(valid, source // 4 * 4 + slot, 0), jnp.where(valid, 1.0, 0.0)

    def lookup_slot(k, core):
        found, source = block_at(owner, x * 4 + zh * 2 + core, (y + k) % 4)
        valid = (found == 1) & (source % 2 == c)
        return jnp.where(valid, source // 2, 0), jnp.where(valid, 1.0, 0.0)

    stages = (None, scatter_near, relay, reduce_half, reduce_side, turn, gather_side, gather_half)
    steps = (None, start_old, spread_old, swap_old, cross_old, finish_old)
    state, olds = {}, {}

    def run(stage, group):
        if stage == 0:
            state[group] = scatter_far(group)
        else:
            state[group] = stages[stage](group, state[group])

    def run_old(step, n):
        if step == 1:
            olds[n] = start_old(n)
        else:
            olds[n] = steps[step](n, olds[n])

    run(0, 0)
    run(1, 0)
    run(0, 1)
    for copy in fetched:
        copy.wait()
    run_old(1, 0)
    old_away = [lookup_old(n, 1 - c) for n in range(8)]
    old_home = [lookup_old(n, c) for n in range(8)]
    for copy in prefetch:
        copy.wait()
    for job in ORDER:
        if job[0] == GRADS:
            run(job[1], job[2])
        else:
            run_old(job[1], job[2])
    kept_old.wait()
    members = lax.fori_loop(0, 16, lambda i, n: n + jnp.where(owner[i] == net.block, 1, 0), jnp.int32(0))
    new[...] = new[...] * jnp.where(members > y, 0.0, 0.6)
    slot_away = [lookup_slot(k, 1 - c) for k in range(4)]
    slot_home = [lookup_slot(k, c) for k in range(4)]
    for relayed, direct, kept in state.values():
        relayed.wait_recv()
        direct.wait_recv()
        kept.wait()

    @pl.when(side == 1)
    def _():
        for a in range(4):
            mat_high[a], mat_low[a] = split(chunk[a].reshape(256, 256).T)

    @pl.when(side == 0)
    def _():
        for a in range(4):
            mat_high[a], mat_low[a] = split(chunk[a].reshape(256, 256))

    def outer(a, b):
        return lax.dot_general(a, b, (((1,), (1,)), ((), ())), preferred_element_type=jnp.float32)

    summed = []
    for part in SETS:
        for n in range(part.start, part.start + part.size):
            i = jnp.where(half == 0, PACKED[0][n][0], PACKED[1][n][0])
            j = jnp.where(half == 0, PACKED[0][n][1], PACKED[1][n][1])
            left_high, right_high = mat_high[i], mat_high[j]
            gram[n] = (
                outer(left_high, mat_low[j]) + outer(mat_low[i], right_high) + outer(left_high, right_high)
            )
        summed.append(
            [
                net.push(gram.at[part, rows_of((y + k) % 4, 64)], ggot.at[k - 1, part], y=k)
                for k in (1, 3, 2)
            ]
        )
    back, on = (x + 3) % 4, (x + 1) % 4
    own, across, first_up, first_down = [], [], [], []
    halved, y_up, y_down, y_far, other_up, other_down, other_far, own_piece = [], [], [], [], [], [], [], []
    for n, part in enumerate(SETS):
        if n < 2:
            olds[n][0].wait()
            for copy in olds[n][1]:
                copy.wait_recv()
        for copy in summed[n]:
            copy.wait_recv()
        piece[part] = 0.6 * oldp[part] + (1.0 - 0.6) * (
            gram[part, rows_of(y, 64)] + ggot[0, part] + ggot[1, part] + ggot[2, part]
        )
        here, there = columns[n].at[x * 2 + zh], sall.at[half, part, y]
        halved.append(net.push(piece.at[part], there, half=1))
        across.append(net.push(piece.at[part], here, zh=1))
        first_up.append(net.push(piece.at[part], here, x=1))
        first_down.append(net.push(piece.at[part], here, x=3))
        y_up.append(net.push(piece.at[part], there, y=1))
        y_down.append(net.push(piece.at[part], there, y=3))
        own.append(net.move(piece.at[part], here))
        own_piece.append(net.move(piece.at[part], there))

    first_far, second_up, second_down, second_far = [], [], [], []

    def pass_first(n):
        first_up[n].wait_recv()
        there = columns[n].at[back * 2 + zh]
        first_far.append(net.push(there, there, x=1))

    def start_second(n):
        across[n].wait_recv()
        there = columns[n].at[x * 2 + 1 - zh]
        second_down.append(net.push(there, there, x=3))
        second_up.append(net.push(there, there, x=1))

    def pass_second(n):
        second_down[n].wait_recv()
        there = columns[n].at[on * 2 + 1 - zh]
        second_far.append(net.push(there, there, x=3))

    def choose(n):
        own[n].wait()
        for copy in (first_down[n], first_far[n], second_up[n], second_far[n]):
            copy.wait_recv()
        swapped = {}
        for k in (2, 1, 3, 0):
            index, mask = slot_away[k]
            leave[n][k] = columns[n][index] * mask
            swapped[k] = net.push(leave[n].at[k], enter[n].at[k], c=1)
        sent = {}
        for k in (2, 1, 3, 0):
            index, mask = slot_home[k]
            ready[n][k] = columns[n][index] * mask
            swapped[k].wait_recv()
            ready[n][k] = ready[n][k] + enter[n][k]
            here = parts.at[SETS[n], y]
            if k:
                sent[k] = net.push(ready[n].at[k], here, y=k)
            else:
                kept = net.move(ready[n].at[0], here)
        return sent, kept

    def pass_own(n):
        y_up[n].wait_recv()
        there = sall.at[half, SETS[n], below]
        y_far.append(net.push(there, there, y=1))

    def start_other(n):
        halved[n].wait_recv()
        there = sall.at[1 - half, SETS[n], y]
        other_down.append(net.push(there, there, y=3))
        other_up.append(net.push(there, there, y=1))

    def pass_other(n):
        other_down[n].wait_recv()
        there = sall.at[1 - half, SETS[n], above]
        other_far.append(net.push(there, there, y=3))

    pass_first(0)
    pass_own(0)
    start_other(0)
    start_second(0)
    pass_first(1)
    pass_own(1)
    start_other(1)
    pass_second(0)
    pass_other(0)
    pass_first(2)
    pass_own(2)
    start_second(1)
    start_other(2)
    pass_other(1)
    sent = [choose(0)]
    pass_second(1)
    start_second(2)
    pass_other(2)
    sent.append(choose(1))
    pass_second(2)

    halves = []
    for k in (0, 1, 3, 2):
        if k:
            sent[0][0][k].wait_recv()
        else:
            sent[0][1].wait()
        at = (y + 4 - k) % 4
        halves.append(net.push(parts.at[SETS[0], at], crossed.at[:, at], half=1))

    for n in range(3):
        own_piece[n].wait()
        for copy in (y_down[n], y_far[n], other_up[n], other_far[n]):
            copy.wait_recv()
    for h in range(2):
        for n in range(5):
            i, j = PACKED[h][n]
            stat[pl.ds(i * 256, 256), pl.ds(j * 256, 256)] = sall[h, n].reshape(256, 256)
    for i, j in ((0, 1), (0, 2), (0, 3), (2, 1), (3, 1), (2, 3)):
        stat[pl.ds(j * 256, 256), pl.ds(i * 256, 256)] = stat[pl.ds(i * 256, 256), pl.ds(j * 256, 256)].T
    top = top_value(stat, column)
    sent.append(choose(2))
    find_root((y, zl), top, stat, rootbuf, base, high, low)
    returned = net.push(rootbuf.at[1], roots.at[side], side=1)
    kept = net.move(rootbuf.at[0], roots.at[side])

    for n in (1, 2):
        sent[n][1].wait()
        for k in (1, 3, 2):
            sent[n][0][k].wait_recv()
    for copy in halves:
        copy.wait_recv()

    def put(i, j, values):
        rows, cols = pl.ds(i * 256, 256), pl.ds(j * 256, 256)
        new[rows, cols] = new[rows, cols] + values

    def part(n):
        return parts[n].reshape(256, 256)

    def turned_part(n):
        return crossed[n].reshape(256, 256).T

    @pl.when(half == 0)
    def _():
        put(0, 0, part(2))
        put(0, 1, part(3))
        put(0, 2, part(0))
        put(0, 3, part(1))
        put(1, 0, part(3).T)
        put(1, 1, part(4))
        put(1, 2, turned_part(0))
        put(1, 3, turned_part(1))

    @pl.when(half == 1)
    def _():
        put(0, 0, turned_part(0))
        put(0, 1, part(0))
        put(0, 2, part(2))
        put(0, 3, part(3))
        put(1, 0, turned_part(1))
        put(1, 1, part(1))
        put(1, 2, part(3).T)
        put(1, 3, part(4))

    written = net.move(new, new_out)
    kept.wait()
    returned.wait_recv()
    written.wait()
    net.close()


def f32(*shape):
    return jax.ShapeDtypeStruct(shape, jnp.float32)


def refresh(owner, grads, old):
    strips, rows = (GROUPS, 4, SUB, BS), (GROUPS, 2, SUB, BS)
    piece = (5, 64, 256)
    scratch = [strips, strips, strips, strips, (GROUPS, 2, 2, SUB, BS), rows, rows, (GROUPS, SUB, BS)]
    scratch += [(2, 64, BS), (2, 64, BS), (4, 64, BS), (5, 256, 256), (4, *piece), piece]
    scratch += [(2, GROUPS, 4, SUB, 256), (4, 4, 64, 256), (5, 256, 256), (3, *piece), (2, 5, 4, 64, 256)]
    scratch += [(BS, BS), (BS, 1), (BS, BS), (2, 64, BS)]
    scratch += [piece, (5, 4, 64, 256), (2, 4, 64, 256), (512, BS)]
    for count in (16, 8, 8, 8, 4, 4):
        scratch += [(count, part.size, 16, 256) for part in OLD_SETS]
    for count in (8, 4, 4, 4):
        scratch += [(count, part.size, 64, 256) for part in SETS]
    halves = [(4, 256, 256), (4, 256, 256), (BS, BS), (BS, BS)]
    out_shape = (f32(512, BS), f32(2, 64, BS))
    return pl.pallas_call(
        refresh_kernel,
        out_shape=out_shape,
        in_specs=[pl.BlockSpec(memory_space=pltpu.SMEM)] + [pl.BlockSpec(memory_space=pl.ANY)] * 2,
        out_specs=tuple(pl.BlockSpec(memory_space=pl.ANY) for _ in out_shape),
        scratch_shapes=[pltpu.VMEM(shape, jnp.float32) for shape in scratch]
        + [pltpu.VMEM(shape, jnp.bfloat16) for shape in halves]
        + [
            pltpu.SemaphoreType.DMA((192,)),
            pltpu.SemaphoreType.DMA((192,)),
            pltpu.SemaphoreType.DMA((48,)),
        ],
        compiler_params=pltpu.CompilerParams(
            collective_id=0, has_side_effects=True, vmem_limit_bytes=VMEM_LIMIT
        ),
    )(owner, grads, old)


def per_device(grads, owner, stats):
    new, roots = refresh(owner, grads.reshape(4, 4, 64, BS), stats[0, 0])
    return new[None, None], roots[None]


def solution(mesh):
    return jax.shard_map(
        per_device,
        mesh=mesh,
        in_specs=(P("dp", "block", None, None), P(), P("block", "dp", None, None)),
        out_specs=(P("block", "dp", None, None), P("block", None, "dp", None)),
        check_vma=False,
    )
```

```python
import jax
import jax.numpy as jnp
from jax import lax
from jax.experimental import pallas as pl
from jax.experimental.pallas import tpu as pltpu
from jax.sharding import PartitionSpec as P

PSTEPS = 8
BS = 1024
GROUPS = 8
SUB = 64 // GROUPS
MESH = pl.DeviceIdType.MESH
VMEM_LIMIT = 60 * 1024 * 1024

PACKED = (
    ((0, 2), (0, 3), (0, 0), (0, 1), (1, 1)),
    ((2, 1), (3, 1), (2, 2), (2, 3), (3, 3)),
)
OLD_SETS = (pl.ds(0, 2), pl.ds(2, 3))
SETS = (pl.ds(0, 2), pl.ds(2, 2), pl.ds(4, 1))


GRADS, OLD = 0, 1
ORDER = (
    (OLD, 1, 0), (GRADS, 0, 2), (GRADS, 1, 2), (GRADS, 2, 0), (GRADS, 0, 3), (GRADS, 1, 3), (GRADS, 2, 1),
    (OLD, 2, 0), (GRADS, 0, 4), (GRADS, 1, 4), (GRADS, 2, 2), (GRADS, 3, 0), (GRADS, 0, 5), (GRADS, 1, 5),
    (GRADS, 2, 3), (OLD, 3, 0), (GRADS, 4, 0), (GRADS, 3, 1), (GRADS, 0, 6), (GRADS, 1, 6), (OLD, 4, 0),
    (GRADS, 5, 0), (GRADS, 2, 4), (GRADS, 4, 1), (GRADS, 3, 2), (GRADS, 0, 7), (GRADS, 1, 7), (GRADS, 2, 5),
    (GRADS, 3, 3), (OLD, 5, 0), (GRADS, 5, 1), (GRADS, 2, 6), (GRADS, 6, 0), (GRADS, 4, 2), (GRADS, 3, 4),
    (GRADS, 4, 3), (GRADS, 7, 0), (GRADS, 2, 7), (GRADS, 5, 2), (OLD, 1, 1), (GRADS, 3, 5), (GRADS, 6, 1),
    (GRADS, 4, 4), (GRADS, 3, 6), (GRADS, 5, 3), (GRADS, 3, 7), (GRADS, 6, 2), (GRADS, 4, 5), (GRADS, 7, 1),
    (GRADS, 5, 4), (GRADS, 4, 6), (GRADS, 4, 7), (GRADS, 7, 2), (OLD, 2, 1), (GRADS, 6, 3), (GRADS, 6, 4),
    (GRADS, 5, 5), (GRADS, 5, 6), (GRADS, 6, 5), (GRADS, 5, 7), (GRADS, 6, 6), (GRADS, 7, 3), (GRADS, 6, 7),
    (GRADS, 7, 4), (GRADS, 7, 5), (OLD, 3, 1), (GRADS, 7, 6), (GRADS, 7, 7), (OLD, 4, 1), (OLD, 5, 1),
)


def place(dp, block):
    return dp // 4, dp % 4, block // 4, block // 2 % 2, block % 2


class Network:
    def __init__(self, send, recv, local):
        self.send, self.recv, self.local = send, recv, local
        self.count = self.locals = 0
        self.sent = []
        self.dp, self.block = lax.axis_index("dp"), lax.axis_index("block")
        self.y, self.zl, self.x, self.zh, self.c = place(self.dp, self.block)

    def device(self, y=0, zl=0, x=0, zh=0, c=0, half=0, side=0):
        row = (self.zl + zl) % 4
        if half:
            row = row + 1 - 2 * (row % 2)
        if side:
            row = (row + 2) % 4
        return (
            (self.y + y) % 4 * 4 + row,
            (self.x + x) % 4 * 4 + (self.zh + zh) % 2 * 2 + (self.c + c) % 2,
        )

    def greet(self, steps):
        barrier = pltpu.get_barrier_semaphore()
        for step in steps:
            pl.semaphore_signal(barrier, inc=1, device_id=self.device(**step), device_id_type=MESH)
        pl.semaphore_wait(barrier, len(steps))

    def push(self, source, target, **step):
        n = self.count
        self.count += 1
        copy = pltpu.make_async_remote_copy(
            src_ref=source,
            dst_ref=target,
            send_sem=self.send.at[n],
            recv_sem=self.recv.at[n],
            device_id=self.device(**step),
            device_id_type=MESH,
        )
        copy.start()
        self.sent.append(copy)
        return copy

    def move(self, source, target):
        copy = pltpu.make_async_copy(source, target, self.local.at[self.locals])
        self.locals += 1
        copy.start()
        return copy

    def close(self):
        for copy in self.sent:
            copy.wait_send()


def split(values):
    high = values.astype(jnp.bfloat16)
    return high, (values - high.astype(jnp.float32)).astype(jnp.bfloat16)


def rank_of(owner, block):
    mine = owner[block]
    count = lax.fori_loop(
        0, 16, lambda i, n: n + jnp.where((i < block) & (owner[i] == mine), 1, 0), jnp.int32(0)
    )
    return mine, count


def block_at(owner, column, wanted):
    def step(i, carry):
        count, found, source = carry
        hit = owner[i] == column
        here = hit & (count == wanted)
        return count + jnp.where(hit, 1, 0), jnp.where(here, 1, found), jnp.where(here, i, source)

    zero = jnp.int32(0)
    _, found, source = lax.fori_loop(0, 16, step, (zero, zero, zero))
    return found, source


def top_value(stat, column):

    def to_column(row):
        for i in range(8):
            rows = pl.ds(i * 128, 128)
            column[rows, :] = jnp.sum(stat[rows, :] * row, axis=1, keepdims=True)
        return column[...]

    def to_row(values):
        column[...] = values
        total = jnp.zeros((8, BS), jnp.float32)
        for i in range(8):
            rows = pl.ds(i * 128, 128)
            total = total + jnp.sum((stat[rows, :] * column[rows, :]).reshape(16, 8, BS), axis=0)
        return jnp.sum(total, axis=0, keepdims=True)

    def norm(values):
        return jnp.sqrt(jnp.sum(values * values, axis=(0, 1), keepdims=True))

    row = jnp.full((1, BS), BS ** (-0.5), jnp.float32)
    for _ in range(PSTEPS // 2):
        image = to_column(row)
        row = to_row(image * (1.0 / norm(image)))
        row = row * (1.0 / norm(row))
    return norm(to_column(row))


def find_root(spot, top, stat, root, base, high, low):
    y, zl = spot
    scale = 2.5 / top
    fourth = jnp.sqrt(jnp.sqrt(scale))

    @pl.loop(0, 4)
    def _(i):
        rows = pl.ds(pl.multiple_of(i * 256, 256), 256)
        eye = lax.broadcasted_iota(jnp.int32, (256, BS), 0) + i * 256 == lax.broadcasted_iota(
            jnp.int32, (256, BS), 1
        )
        values = (jnp.where(eye, 5.0, 0.0) - scale * stat[rows, :]) / 4.0
        base[rows, :] = values
        upper, lower = split(values)
        high[rows, :] = upper
        low[rows, :] = lower

    def times(left):
        upper, lower = split(left)

        def product(a, b):
            return jnp.dot(a, b, preferred_element_type=jnp.float32)

        both = product(jnp.concatenate([upper, lower], axis=0), high[...])
        return both[128:] + product(upper, low[...]) + both[:128]

    own = pl.multiple_of((y * 4 + zl) * 64, 64)
    other = pl.multiple_of((y * 4 + (zl + 2) % 4) * 64, 64)
    first = jnp.concatenate([base[pl.ds(own, 64), :], base[pl.ds(other, 64), :]], axis=0)
    power = times(times(times(first)))
    result = (5.0 * first + times(4.0 * times(power) - 5.0 * power)) * (fourth / 4.0)
    root[0] = result[:64]
    root[1] = result[64:]


def refresh_kernel(owner, grads, old, new_out, roots, *scratch):
    far, up, down, stage, mine, middle, first_got, second_got, toward, away, home = scratch[:11]
    packed, slots, oldp, both, chunk, gram, ggot, sall, stat, column, base, rootbuf = scratch[11:23]
    piece, parts, crossed, new = scratch[23:27]
    spread, outgo, income, near, cross, fin = (scratch[27 + 2 * n : 29 + 2 * n] for n in range(6))
    columns, leave, enter, ready = (scratch[39 + 3 * n : 42 + 3 * n] for n in range(4))
    mat_high, mat_low, high, low = scratch[51:55]
    net = Network(*scratch[55:])
    y, zl, x, zh, c = net.y, net.zl, net.x, net.zh, net.c
    side, half = zl // 2, zl % 2
    below, above, beyond = (y + 3) % 4, (y + 1) % 4, (y + 2) % 4

    def rows_of(at, size):
        return pl.ds(pl.multiple_of(at * size, size), size)

    def strip(ref, chunk_at, first, group):
        return ref.at[chunk_at, pl.ds(first, 2), pl.ds(group * SUB, SUB)]

    fetched = []
    for n in range(5):
        i = jnp.where(half == 0, PACKED[0][n][0], PACKED[1][n][0] - 2)
        j = jnp.where(half == 0, PACKED[0][n][1], PACKED[1][n][1])
        fetched.append(net.move(old.at[rows_of(i, 256), rows_of(j, 256)], packed.at[n]))
    prefetch = [
        net.move(grads.at[above, pl.ds(0, 2)], toward),
        net.move(grads.at[below, pl.ds(2, 2)], away),
        net.move(grads.at[y], home),
    ]
    kept_old = net.move(old, new)
    net.greet(
        [dict(y=1), dict(y=2), dict(y=3), dict(half=1), dict(side=1)]
        + [dict(x=1), dict(x=2), dict(x=3), dict(zh=1), dict(c=1)]
    )

    def scatter_far(group):
        far_up = net.push(strip(grads, beyond, 0, group), far.at[group, pl.ds(0, 2)], y=1)
        far_down = net.push(strip(grads, beyond, 2, group), far.at[group, pl.ds(2, 2)], y=3)
        return far_up, far_down

    def scatter_near(group, copies):
        near_up = net.push(strip(grads, above, 2, group), up.at[group, pl.ds(2, 2)], y=1)
        near_down = net.push(strip(grads, below, 0, group), down.at[group, pl.ds(0, 2)], y=3)
        return *copies, near_up, near_down

    def relay(group, copies):
        rows = pl.ds(group * SUB, SUB)
        copies[0].wait_recv()
        stage[group, 0:2] = far[group, 0:2] + toward[:, rows]
        first = net.push(stage.at[group, pl.ds(0, 2)], up.at[group, pl.ds(0, 2)], y=1)
        copies[1].wait_recv()
        stage[group, 2:4] = far[group, 2:4] + away[:, rows]
        second = net.push(stage.at[group, pl.ds(2, 2)], down.at[group, pl.ds(2, 2)], y=3)
        return first, second, copies[2], copies[3]

    def reduce_half(group, copies):
        for copy in copies:
            copy.wait_recv()
        for n in range(4):
            mine[group, n % 2, n // 2] = home[n, pl.ds(group * SUB, SUB)] + up[group, n] + down[group, n]
        return net.push(mine.at[group, 1 - half], first_got.at[group], half=1)

    def reduce_side(group, copy):
        copy.wait_recv()
        middle[group] = mine[group, half] + first_got[group]
        return net.push(middle.at[group, 1 - side], second_got.at[group], side=1)

    def turn(group, copy):
        copy.wait_recv()
        total = middle[group, side] + second_got[group]
        for a in range(4):
            both[1, group, a] = total[:, a * 256 : (a + 1) * 256]
        kept = net.move(both.at[1, group, y], both.at[0, group, y])
        return [net.push(both.at[1, group, (y + k) % 4], both.at[0, group, y], y=k) for k in (1, 3, 2)], kept

    def rows_in(device, group):
        return chunk.at[:, device, pl.ds(group * SUB, SUB)]

    def gather_side(group, turned):
        copies, kept = turned
        for copy in copies:
            copy.wait_recv()
        kept.wait()
        here = rows_in(zl, group)
        from_side = net.push(both.at[1 - side, group], here, side=1)
        from_half = net.push(both.at[side, group], here, half=1)
        return from_side, from_half, net.move(both.at[side, group], here)

    def gather_half(group, copies):
        copies[0].wait_recv()
        there = rows_in((zl + 2) % 4, group)
        return net.push(there, there, half=1), copies[1], copies[2]

    def start_old(n):
        part = OLD_SETS[n]
        own = net.move(packed.at[part, rows_of(y, 64)], slots.at[y, part])
        return own, {
            k: net.push(packed.at[part, rows_of((y + k) % 4, 64)], slots.at[y, part], y=k) for k in (1, 3, 2)
        }

    def spread_old(n, started):
        own, slotted = started
        local, remote = [], []
        for k in (0, 1, 3, 2):
            if k == 0:
                own.wait()
            else:
                slotted[k].wait_recv()
            at = (y + 4 - k) % 4
            for m in (0, 1, 2, 3):
                source = slots.at[at, OLD_SETS[n], rows_of((x + m) % 4, 16)]
                if m == 0:
                    local.append(net.move(source, spread[n].at[x * 4 + at]))
                else:
                    remote.append(net.push(source, spread[n].at[x * 4 + at], x=m))
        return local, remote

    def swap_old(n, spreads):
        for copy in spreads[0]:
            copy.wait()
        for copy in spreads[1]:
            copy.wait_recv()
        for i, (index, mask) in enumerate(old_away):
            outgo[n][i] = spread[n][index] * mask
        return net.push(outgo[n], income[n], c=1)

    def cross_old(n, swapped):
        for i, (index, mask) in enumerate(old_home):
            near[n][i] = spread[n][index] * mask
        swapped.wait_recv()
        for i in range(8):
            near[n][i] = near[n][i] + income[n][i]
        return net.push(near[n].at[pl.ds(4, 4)], cross[n], zh=1)

    def finish_old(n, crossing):
        crossing.wait_recv()
        for i in range(4):
            fin[n][i] = near[n][i] + cross[n][i]
        here = oldp.at[OLD_SETS[n], rows_of(x, 16)]
        own = net.move(fin[n].at[0], here)
        return own, [net.push(fin[n].at[m], here, x=m) for m in (1, 2, 3)]

    def lookup_old(n, core):
        target = (x + n % 4) % 4 * 4 + (zh + n // 4) % 2 * 2 + core
        source, slot = rank_of(owner, target)
        valid = (source // 2 % 2 == zh) & (source % 2 == c)
        return jnp.where(valid, source // 4 * 4 + slot, 0), jnp.where(valid, 1.0, 0.0)

    def lookup_slot(k, core):
        found, source = block_at(owner, x * 4 + zh * 2 + core, (y + k) % 4)
        valid = (found == 1) & (source % 2 == c)
        return jnp.where(valid, source // 2, 0), jnp.where(valid, 1.0, 0.0)

    stages = (None, scatter_near, relay, reduce_half, reduce_side, turn, gather_side, gather_half)
    steps = (None, start_old, spread_old, swap_old, cross_old, finish_old)
    state, olds = {}, {}

    def run(stage, group):
        if stage == 0:
            state[group] = scatter_far(group)
        else:
            state[group] = stages[stage](group, state[group])

    def run_old(step, n):
        if step == 1:
            olds[n] = start_old(n)
        else:
            olds[n] = steps[step](n, olds[n])

    run(0, 0)
    run(1, 0)
    run(0, 1)
    run(1, 1)
    for copy in fetched:
        copy.wait()
    old_away = [lookup_old(n, 1 - c) for n in range(8)]
    old_home = [lookup_old(n, c) for n in range(8)]
    for copy in prefetch:
        copy.wait()
    for job in ORDER:
        if job[0] == GRADS:
            run(job[1], job[2])
        else:
            run_old(job[1], job[2])
    kept_old.wait()
    members = lax.fori_loop(0, 16, lambda i, n: n + jnp.where(owner[i] == net.block, 1, 0), jnp.int32(0))
    new[...] = new[...] * jnp.where(members > y, 0.0, 0.6)
    slot_away = [lookup_slot(k, 1 - c) for k in range(4)]
    slot_home = [lookup_slot(k, c) for k in range(4)]
    for relayed, direct, kept in state.values():
        relayed.wait_recv()
        direct.wait_recv()
        kept.wait()

    @pl.when(side == 1)
    def _():
        for a in range(4):
            mat_high[a], mat_low[a] = split(chunk[a].reshape(256, 256).T)

    @pl.when(side == 0)
    def _():
        for a in range(4):
            mat_high[a], mat_low[a] = split(chunk[a].reshape(256, 256))

    def outer(a, b):
        return lax.dot_general(a, b, (((1,), (1,)), ((), ())), preferred_element_type=jnp.float32)

    summed = []
    for part in SETS:
        for n in range(part.start, part.start + part.size):
            i = jnp.where(half == 0, PACKED[0][n][0], PACKED[1][n][0])
            j = jnp.where(half == 0, PACKED[0][n][1], PACKED[1][n][1])
            left_high, right_high = mat_high[i], mat_high[j]
            gram[n] = (
                outer(left_high, mat_low[j]) + outer(mat_low[i], right_high) + outer(left_high, right_high)
            )
        summed.append(
            [
                net.push(gram.at[part, rows_of((y + k) % 4, 64)], ggot.at[k - 1, part], y=k)
                for k in (1, 3, 2)
            ]
        )
    back, on = (x + 3) % 4, (x + 1) % 4
    own, across, first_up, first_down = [], [], [], []
    halved, y_up, y_down, y_far, other_up, other_down, other_far, own_piece = [], [], [], [], [], [], [], []
    for n, part in enumerate(SETS):
        if n < 2:
            olds[n][0].wait()
            for copy in olds[n][1]:
                copy.wait_recv()
        for copy in summed[n]:
            copy.wait_recv()
        piece[part] = 0.6 * oldp[part] + (1.0 - 0.6) * (
            gram[part, rows_of(y, 64)] + ggot[0, part] + ggot[1, part] + ggot[2, part]
        )
        here, there = columns[n].at[x * 2 + zh], sall.at[half, part, y]
        halved.append(net.push(piece.at[part], there, half=1))
        across.append(net.push(piece.at[part], here, zh=1))
        first_up.append(net.push(piece.at[part], here, x=1))
        first_down.append(net.push(piece.at[part], here, x=3))
        y_up.append(net.push(piece.at[part], there, y=1))
        y_down.append(net.push(piece.at[part], there, y=3))
        own.append(net.move(piece.at[part], here))
        own_piece.append(net.move(piece.at[part], there))

    first_far, second_up, second_down, second_far = [], [], [], []

    def pass_first(n):
        first_up[n].wait_recv()
        there = columns[n].at[back * 2 + zh]
        first_far.append(net.push(there, there, x=1))

    def start_second(n):
        across[n].wait_recv()
        there = columns[n].at[x * 2 + 1 - zh]
        second_down.append(net.push(there, there, x=3))
        second_up.append(net.push(there, there, x=1))

    def pass_second(n):
        second_down[n].wait_recv()
        there = columns[n].at[on * 2 + 1 - zh]
        second_far.append(net.push(there, there, x=3))

    def choose(n):
        own[n].wait()
        for copy in (first_down[n], first_far[n], second_up[n], second_far[n]):
            copy.wait_recv()
        swapped = {}
        for k in (2, 1, 3, 0):
            index, mask = slot_away[k]
            leave[n][k] = columns[n][index] * mask
            swapped[k] = net.push(leave[n].at[k], enter[n].at[k], c=1)
        sent = {}
        for k in (2, 1, 3, 0):
            index, mask = slot_home[k]
            ready[n][k] = columns[n][index] * mask
            swapped[k].wait_recv()
            ready[n][k] = ready[n][k] + enter[n][k]
            here = parts.at[SETS[n], y]
            if k:
                sent[k] = net.push(ready[n].at[k], here, y=k)
            else:
                kept = net.move(ready[n].at[0], here)
        return sent, kept

    def pass_own(n):
        y_up[n].wait_recv()
        there = sall.at[half, SETS[n], below]
        y_far.append(net.push(there, there, y=1))

    def start_other(n):
        halved[n].wait_recv()
        there = sall.at[1 - half, SETS[n], y]
        other_down.append(net.push(there, there, y=3))
        other_up.append(net.push(there, there, y=1))

    def pass_other(n):
        other_down[n].wait_recv()
        there = sall.at[1 - half, SETS[n], above]
        other_far.append(net.push(there, there, y=3))

    pass_first(0)
    pass_own(0)
    start_other(0)
    start_second(0)
    pass_first(1)
    pass_own(1)
    start_other(1)
    pass_second(0)
    pass_other(0)
    pass_first(2)
    pass_own(2)
    start_second(1)
    start_other(2)
    pass_other(1)
    sent = [choose(0)]
    pass_second(1)
    start_second(2)
    pass_other(2)
    sent.append(choose(1))
    pass_second(2)

    halves = []
    for k in (0, 1, 3, 2):
        if k:
            sent[0][0][k].wait_recv()
        else:
            sent[0][1].wait()
        at = (y + 4 - k) % 4
        halves.append(net.push(parts.at[SETS[0], at], crossed.at[:, at], half=1))

    for n in range(3):
        own_piece[n].wait()
        for copy in (y_down[n], y_far[n], other_up[n], other_far[n]):
            copy.wait_recv()
    for h in range(2):
        for n in range(5):
            i, j = PACKED[h][n]
            stat[pl.ds(i * 256, 256), pl.ds(j * 256, 256)] = sall[h, n].reshape(256, 256)
    for i, j in ((0, 1), (0, 2), (0, 3), (2, 1), (3, 1), (2, 3)):
        stat[pl.ds(j * 256, 256), pl.ds(i * 256, 256)] = stat[pl.ds(i * 256, 256), pl.ds(j * 256, 256)].T
    top = top_value(stat, column)
    sent.append(choose(2))
    find_root((y, zl), top, stat, rootbuf, base, high, low)
    returned = net.push(rootbuf.at[1], roots.at[side], side=1)
    kept = net.move(rootbuf.at[0], roots.at[side])

    for n in (1, 2):
        sent[n][1].wait()
        for k in (1, 3, 2):
            sent[n][0][k].wait_recv()
    for copy in halves:
        copy.wait_recv()

    def put(i, j, values):
        rows, cols = pl.ds(i * 256, 256), pl.ds(j * 256, 256)
        new[rows, cols] = new[rows, cols] + values

    def part(n):
        return parts[n].reshape(256, 256)

    def turned_part(n):
        return crossed[n].reshape(256, 256).T

    @pl.when(half == 0)
    def _():
        put(0, 0, part(2))
        put(0, 1, part(3))
        put(0, 2, part(0))
        put(0, 3, part(1))
        put(1, 0, part(3).T)
        put(1, 1, part(4))
        put(1, 2, turned_part(0))
        put(1, 3, turned_part(1))

    @pl.when(half == 1)
    def _():
        put(0, 0, turned_part(0))
        put(0, 1, part(0))
        put(0, 2, part(2))
        put(0, 3, part(3))
        put(1, 0, turned_part(1))
        put(1, 1, part(1))
        put(1, 2, part(3).T)
        put(1, 3, part(4))

    written = net.move(new, new_out)
    kept.wait()
    returned.wait_recv()
    written.wait()
    net.close()


def f32(*shape):
    return jax.ShapeDtypeStruct(shape, jnp.float32)


def refresh(owner, grads, old):
    strips, rows = (GROUPS, 4, SUB, BS), (GROUPS, 2, SUB, BS)
    piece = (5, 64, 256)
    scratch = [strips, strips, strips, strips, (GROUPS, 2, 2, SUB, BS), rows, rows, (GROUPS, SUB, BS)]
    scratch += [(2, 64, BS), (2, 64, BS), (4, 64, BS), (5, 256, 256), (4, *piece), piece]
    scratch += [(2, GROUPS, 4, SUB, 256), (4, 4, 64, 256), (5, 256, 256), (3, *piece), (2, 5, 4, 64, 256)]
    scratch += [(BS, BS), (BS, 1), (BS, BS), (2, 64, BS)]
    scratch += [piece, (5, 4, 64, 256), (2, 4, 64, 256), (512, BS)]
    for count in (16, 8, 8, 8, 4, 4):
        scratch += [(count, part.size, 16, 256) for part in OLD_SETS]
    for count in (8, 4, 4, 4):
        scratch += [(count, part.size, 64, 256) for part in SETS]
    halves = [(4, 256, 256), (4, 256, 256), (BS, BS), (BS, BS)]
    out_shape = (f32(512, BS), f32(2, 64, BS))
    return pl.pallas_call(
        refresh_kernel,
        out_shape=out_shape,
        in_specs=[pl.BlockSpec(memory_space=pltpu.SMEM)] + [pl.BlockSpec(memory_space=pl.ANY)] * 2,
        out_specs=tuple(pl.BlockSpec(memory_space=pl.ANY) for _ in out_shape),
        scratch_shapes=[pltpu.VMEM(shape, jnp.float32) for shape in scratch]
        + [pltpu.VMEM(shape, jnp.bfloat16) for shape in halves]
        + [
            pltpu.SemaphoreType.DMA((256,)),
            pltpu.SemaphoreType.DMA((256,)),
            pltpu.SemaphoreType.DMA((64,)),
        ],
        compiler_params=pltpu.CompilerParams(
            collective_id=0, has_side_effects=True, vmem_limit_bytes=VMEM_LIMIT
        ),
    )(owner, grads, old)


def per_device(grads, owner, stats):
    new, roots = refresh(owner, grads.reshape(4, 4, 64, BS), stats[0, 0])
    return new[None, None], roots[None]


def solution(mesh):
    return jax.shard_map(
        per_device,
        mesh=mesh,
        in_specs=(P("dp", "block", None, None), P(), P("block", "dp", None, None)),
        out_specs=(P("block", "dp", None, None), P("block", None, "dp", None)),
        check_vma=False,
    )
```

```python
import jax
import jax.numpy as jnp
from jax import lax
from jax.experimental import pallas as pl
from jax.experimental.pallas import tpu as pltpu
from jax.sharding import PartitionSpec as P

PSTEPS = 8
BS = 1024
GROUPS = 8
SUB = 64 // GROUPS
MESH = pl.DeviceIdType.MESH
VMEM_LIMIT = 60 * 1024 * 1024

PACKED = (
    ((0, 2), (0, 3), (0, 0), (0, 1), (1, 1)),
    ((2, 1), (3, 1), (2, 2), (2, 3), (3, 3)),
)
OLD_SETS = (pl.ds(0, 2), pl.ds(2, 3))
SETS = (pl.ds(0, 2), pl.ds(2, 2), pl.ds(4, 1))


GRADS, OLD = 0, 1
ORDER = (
    (OLD, 1, 0), (GRADS, 0, 2), (GRADS, 1, 2), (GRADS, 2, 0), (GRADS, 0, 3), (GRADS, 1, 3), (GRADS, 2, 1),
    (OLD, 2, 0), (GRADS, 0, 4), (GRADS, 1, 4), (GRADS, 2, 2), (GRADS, 3, 0), (GRADS, 0, 5), (GRADS, 1, 5),
    (GRADS, 2, 3), (OLD, 3, 0), (GRADS, 4, 0), (GRADS, 3, 1), (GRADS, 0, 6), (GRADS, 1, 6), (OLD, 4, 0),
    (GRADS, 5, 0), (GRADS, 2, 4), (GRADS, 4, 1), (GRADS, 3, 2), (GRADS, 0, 7), (GRADS, 1, 7), (GRADS, 2, 5),
    (GRADS, 3, 3), (OLD, 5, 0), (GRADS, 5, 1), (GRADS, 2, 6), (GRADS, 6, 0), (GRADS, 4, 2), (GRADS, 3, 4),
    (GRADS, 4, 3), (GRADS, 7, 0), (GRADS, 2, 7), (GRADS, 5, 2), (OLD, 1, 1), (GRADS, 3, 5), (GRADS, 6, 1),
    (GRADS, 4, 4), (GRADS, 3, 6), (GRADS, 5, 3), (GRADS, 3, 7), (GRADS, 6, 2), (GRADS, 4, 5), (GRADS, 7, 1),
    (GRADS, 5, 4), (GRADS, 4, 6), (GRADS, 4, 7), (GRADS, 7, 2), (OLD, 2, 1), (GRADS, 6, 3), (GRADS, 6, 4),
    (GRADS, 5, 5), (GRADS, 5, 6), (GRADS, 6, 5), (GRADS, 5, 7), (GRADS, 6, 6), (GRADS, 7, 3), (GRADS, 6, 7),
    (GRADS, 7, 4), (GRADS, 7, 5), (OLD, 3, 1), (GRADS, 7, 6), (GRADS, 7, 7), (OLD, 4, 1), (OLD, 5, 1),
)


def place(dp, block):
    return dp // 4, dp % 4, block // 4, block // 2 % 2, block % 2


class Network:
    def __init__(self, send, recv, local):
        self.send, self.recv, self.local = send, recv, local
        self.count = self.locals = 0
        self.sent = []
        self.dp, self.block = lax.axis_index("dp"), lax.axis_index("block")
        self.y, self.zl, self.x, self.zh, self.c = place(self.dp, self.block)

    def device(self, y=0, zl=0, x=0, zh=0, c=0, half=0, side=0):
        row = (self.zl + zl) % 4
        if half:
            row = row + 1 - 2 * (row % 2)
        if side:
            row = (row + 2) % 4
        return (
            (self.y + y) % 4 * 4 + row,
            (self.x + x) % 4 * 4 + (self.zh + zh) % 2 * 2 + (self.c + c) % 2,
        )

    def greet(self, steps):
        barrier = pltpu.get_barrier_semaphore()
        for step in steps:
            pl.semaphore_signal(barrier, inc=1, device_id=self.device(**step), device_id_type=MESH)
        pl.semaphore_wait(barrier, len(steps))

    def push(self, source, target, **step):
        n = self.count
        self.count += 1
        copy = pltpu.make_async_remote_copy(
            src_ref=source,
            dst_ref=target,
            send_sem=self.send.at[n],
            recv_sem=self.recv.at[n],
            device_id=self.device(**step),
            device_id_type=MESH,
        )
        copy.start()
        self.sent.append(copy)
        return copy

    def move(self, source, target):
        copy = pltpu.make_async_copy(source, target, self.local.at[self.locals])
        self.locals += 1
        copy.start()
        return copy

    def close(self):
        for copy in self.sent:
            copy.wait_send()


def split(values):
    high = values.astype(jnp.bfloat16)
    return high, (values - high.astype(jnp.float32)).astype(jnp.bfloat16)


def rank_of(owner, block):
    mine = owner[block]
    count = lax.fori_loop(
        0, 16, lambda i, n: n + jnp.where((i < block) & (owner[i] == mine), 1, 0), jnp.int32(0)
    )
    return mine, count


def block_at(owner, column, wanted):
    def step(i, carry):
        count, found, source = carry
        hit = owner[i] == column
        here = hit & (count == wanted)
        return count + jnp.where(hit, 1, 0), jnp.where(here, 1, found), jnp.where(here, i, source)

    zero = jnp.int32(0)
    _, found, source = lax.fori_loop(0, 16, step, (zero, zero, zero))
    return found, source


def top_value(stat, column):

    def to_column(row):
        for i in range(8):
            rows = pl.ds(i * 128, 128)
            column[rows, :] = jnp.sum(stat[rows, :] * row, axis=1, keepdims=True)
        return column[...]

    def to_row(values):
        column[...] = values
        total = jnp.zeros((8, BS), jnp.float32)
        for i in range(8):
            rows = pl.ds(i * 128, 128)
            total = total + jnp.sum((stat[rows, :] * column[rows, :]).reshape(16, 8, BS), axis=0)
        return jnp.sum(total, axis=0, keepdims=True)

    def norm(values):
        return jnp.sqrt(jnp.sum(values * values, axis=(0, 1), keepdims=True))

    row = jnp.full((1, BS), BS ** (-0.5), jnp.float32)
    for _ in range(PSTEPS // 2):
        image = to_column(row)
        row = to_row(image * (1.0 / norm(image)))
        row = row * (1.0 / norm(row))
    return norm(to_column(row))


def find_root(spot, top, stat, root, base, high, low):
    y, zl = spot
    scale = 2.5 / top
    fourth = jnp.sqrt(jnp.sqrt(scale))

    @pl.loop(0, 4)
    def _(i):
        rows = pl.ds(pl.multiple_of(i * 256, 256), 256)
        eye = lax.broadcasted_iota(jnp.int32, (256, BS), 0) + i * 256 == lax.broadcasted_iota(
            jnp.int32, (256, BS), 1
        )
        values = (jnp.where(eye, 5.0, 0.0) - scale * stat[rows, :]) / 4.0
        base[rows, :] = values
        upper, lower = split(values)
        high[rows, :] = upper
        low[rows, :] = lower

    def times(left):
        upper, lower = split(left)

        def product(a, b):
            return jnp.dot(a, b, preferred_element_type=jnp.float32)

        both = product(jnp.concatenate([upper, lower], axis=0), high[...])
        return both[128:] + product(upper, low[...]) + both[:128]

    own = pl.multiple_of((y * 4 + zl) * 64, 64)
    other = pl.multiple_of((y * 4 + (zl + 2) % 4) * 64, 64)
    first = jnp.concatenate([base[pl.ds(own, 64), :], base[pl.ds(other, 64), :]], axis=0)
    power = times(times(times(first)))
    result = (5.0 * first + times(4.0 * times(power) - 5.0 * power)) * (fourth / 4.0)
    root[0] = result[:64]
    root[1] = result[64:]


def refresh_kernel(owner, grads, old, new_out, roots, *scratch):
    far, up, down, stage, mine, middle, first_got, second_got, toward, away, home = scratch[:11]
    packed, slots, oldp, both, chunk, gram, ggot, sall, stat, column, base, rootbuf = scratch[11:23]
    piece, parts, crossed, new = scratch[23:27]
    spread, outgo, income, near, cross, fin = (scratch[27 + 2 * n : 29 + 2 * n] for n in range(6))
    columns, leave, enter, ready = (scratch[39 + 3 * n : 42 + 3 * n] for n in range(4))
    mat_high, mat_low, high, low = scratch[51:55]
    net = Network(*scratch[55:])
    y, zl, x, zh, c = net.y, net.zl, net.x, net.zh, net.c
    side, half = zl // 2, zl % 2
    below, above, beyond = (y + 3) % 4, (y + 1) % 4, (y + 2) % 4

    def rows_of(at, size):
        return pl.ds(pl.multiple_of(at * size, size), size)

    def strip(ref, chunk_at, first, group):
        return ref.at[chunk_at, pl.ds(first, 2), pl.ds(group * SUB, SUB)]

    fetched = []
    for n in range(5):
        i = jnp.where(half == 0, PACKED[0][n][0], PACKED[1][n][0] - 2)
        j = jnp.where(half == 0, PACKED[0][n][1], PACKED[1][n][1])
        fetched.append(net.move(old.at[rows_of(i, 256), rows_of(j, 256)], packed.at[n]))
    prefetch = [
        net.move(grads.at[above, pl.ds(0, 2)], toward),
        net.move(grads.at[below, pl.ds(2, 2)], away),
        net.move(grads.at[y], home),
    ]
    kept_old = net.move(old, new)
    net.greet(
        [dict(y=1), dict(y=2), dict(y=3), dict(half=1), dict(side=1)]
        + [dict(x=1), dict(x=2), dict(x=3), dict(zh=1), dict(c=1)]
    )

    def scatter_far(group):
        far_up = net.push(strip(grads, beyond, 0, group), far.at[group, pl.ds(0, 2)], y=1)
        far_down = net.push(strip(grads, beyond, 2, group), far.at[group, pl.ds(2, 2)], y=3)
        return far_up, far_down

    def scatter_near(group, copies):
        near_up = net.push(strip(grads, above, 2, group), up.at[group, pl.ds(2, 2)], y=1)
        near_down = net.push(strip(grads, below, 0, group), down.at[group, pl.ds(0, 2)], y=3)
        return *copies, near_up, near_down

    def relay(group, copies):
        rows = pl.ds(group * SUB, SUB)
        copies[0].wait_recv()
        stage[group, 0:2] = far[group, 0:2] + toward[:, rows]
        first = net.push(stage.at[group, pl.ds(0, 2)], up.at[group, pl.ds(0, 2)], y=1)
        copies[1].wait_recv()
        stage[group, 2:4] = far[group, 2:4] + away[:, rows]
        second = net.push(stage.at[group, pl.ds(2, 2)], down.at[group, pl.ds(2, 2)], y=3)
        return first, second, copies[2], copies[3]

    def reduce_half(group, copies):
        for copy in copies:
            copy.wait_recv()
        for n in range(4):
            mine[group, n % 2, n // 2] = home[n, pl.ds(group * SUB, SUB)] + up[group, n] + down[group, n]
        return net.push(mine.at[group, 1 - half], first_got.at[group], half=1)

    def reduce_side(group, copy):
        copy.wait_recv()
        middle[group] = mine[group, half] + first_got[group]
        return net.push(middle.at[group, 1 - side], second_got.at[group], side=1)

    def turn(group, copy):
        copy.wait_recv()
        total = middle[group, side] + second_got[group]
        for a in range(4):
            both[1, group, a] = total[:, a * 256 : (a + 1) * 256]
        kept = net.move(both.at[1, group, y], both.at[0, group, y])
        return [net.push(both.at[1, group, (y + k) % 4], both.at[0, group, y], y=k) for k in (1, 3, 2)], kept

    def rows_in(device, group):
        return chunk.at[:, device, pl.ds(group * SUB, SUB)]

    def gather_side(group, turned):
        copies, kept = turned
        for copy in copies:
            copy.wait_recv()
        kept.wait()
        here = rows_in(zl, group)
        from_side = net.push(both.at[1 - side, group], here, side=1)
        from_half = net.push(both.at[side, group], here, half=1)
        return from_side, from_half, net.move(both.at[side, group], here)

    def gather_half(group, copies):
        copies[0].wait_recv()
        there = rows_in((zl + 2) % 4, group)
        return net.push(there, there, half=1), copies[1], copies[2]

    def start_old(n):
        part = OLD_SETS[n]
        own = net.move(packed.at[part, rows_of(y, 64)], slots.at[y, part])
        return own, {
            k: net.push(packed.at[part, rows_of((y + k) % 4, 64)], slots.at[y, part], y=k) for k in (1, 3, 2)
        }

    def spread_old(n, started):
        own, slotted = started
        local, remote = [], []
        for k in (0, 1, 3, 2):
            if k == 0:
                own.wait()
            else:
                slotted[k].wait_recv()
            at = (y + 4 - k) % 4
            for m in (0, 1, 2, 3):
                source = slots.at[at, OLD_SETS[n], rows_of((x + m) % 4, 16)]
                if m == 0:
                    local.append(net.move(source, spread[n].at[x * 4 + at]))
                else:
                    remote.append(net.push(source, spread[n].at[x * 4 + at], x=m))
        return local, remote

    def swap_old(n, spreads):
        for copy in spreads[0]:
            copy.wait()
        for copy in spreads[1]:
            copy.wait_recv()
        for i, (index, mask) in enumerate(old_away):
            outgo[n][i] = spread[n][index] * mask
        return net.push(outgo[n], income[n], c=1)

    def cross_old(n, swapped):
        for i, (index, mask) in enumerate(old_home):
            near[n][i] = spread[n][index] * mask
        swapped.wait_recv()
        for i in range(8):
            near[n][i] = near[n][i] + income[n][i]
        return net.push(near[n].at[pl.ds(4, 4)], cross[n], zh=1)

    def finish_old(n, crossing):
        crossing.wait_recv()
        for i in range(4):
            fin[n][i] = near[n][i] + cross[n][i]
        here = oldp.at[OLD_SETS[n], rows_of(x, 16)]
        own = net.move(fin[n].at[0], here)
        return own, [net.push(fin[n].at[m], here, x=m) for m in (1, 2, 3)]

    def lookup_old(n, core):
        target = (x + n % 4) % 4 * 4 + (zh + n // 4) % 2 * 2 + core
        source, slot = rank_of(owner, target)
        valid = (source // 2 % 2 == zh) & (source % 2 == c)
        return jnp.where(valid, source // 4 * 4 + slot, 0), jnp.where(valid, 1.0, 0.0)

    def lookup_slot(k, core):
        found, source = block_at(owner, x * 4 + zh * 2 + core, (y + k) % 4)
        valid = (found == 1) & (source % 2 == c)
        return jnp.where(valid, source // 2, 0), jnp.where(valid, 1.0, 0.0)

    stages = (None, scatter_near, relay, reduce_half, reduce_side, turn, gather_side, gather_half)
    steps = (None, start_old, spread_old, swap_old, cross_old, finish_old)
    state, olds = {}, {}

    def run(stage, group):
        if stage == 0:
            state[group] = scatter_far(group)
        else:
            state[group] = stages[stage](group, state[group])

    def run_old(step, n):
        if step == 1:
            olds[n] = start_old(n)
        else:
            olds[n] = steps[step](n, olds[n])

    run(0, 0)
    run(1, 0)
    run(0, 1)
    run(1, 1)
    for copy in fetched:
        copy.wait()
    old_away = [lookup_old(n, 1 - c) for n in range(8)]
    old_home = [lookup_old(n, c) for n in range(8)]
    for copy in prefetch:
        copy.wait()
    for job in ORDER:
        if job[0] == GRADS:
            run(job[1], job[2])
        else:
            run_old(job[1], job[2])
    kept_old.wait()
    members = lax.fori_loop(0, 16, lambda i, n: n + jnp.where(owner[i] == net.block, 1, 0), jnp.int32(0))
    new[...] = new[...] * jnp.where(members > y, 0.0, 0.6)
    slot_away = [lookup_slot(k, 1 - c) for k in range(4)]
    slot_home = [lookup_slot(k, c) for k in range(4)]
    for relayed, direct, kept in state.values():
        relayed.wait_recv()
        direct.wait_recv()
        kept.wait()

    @pl.when(side == 1)
    def _():
        for a in range(4):
            mat_high[a], mat_low[a] = split(chunk[a].reshape(256, 256).T)

    @pl.when(side == 0)
    def _():
        for a in range(4):
            mat_high[a], mat_low[a] = split(chunk[a].reshape(256, 256))

    def outer(a, b):
        return lax.dot_general(a, b, (((1,), (1,)), ((), ())), preferred_element_type=jnp.float32)

    summed = []
    for part in SETS:
        for n in range(part.start, part.start + part.size):
            i = jnp.where(half == 0, PACKED[0][n][0], PACKED[1][n][0])
            j = jnp.where(half == 0, PACKED[0][n][1], PACKED[1][n][1])
            left_high, right_high = mat_high[i], mat_high[j]
            gram[n] = (
                outer(left_high, mat_low[j]) + outer(mat_low[i], right_high) + outer(left_high, right_high)
            )
        summed.append(
            [
                net.push(gram.at[part, rows_of((y + k) % 4, 64)], ggot.at[k - 1, part], y=k)
                for k in (1, 3, 2)
            ]
        )
    back, on = (x + 3) % 4, (x + 1) % 4
    own, across, first_up, first_down = [], {}, [], []
    halved, y_up, y_down, y_far, other_up, other_down, other_far, own_piece = [], [], [], [], [], [], [], []
    for n, part in enumerate(SETS):
        if n < 2:
            olds[n][0].wait()
            for copy in olds[n][1]:
                copy.wait_recv()
        for copy in summed[n]:
            copy.wait_recv()
        piece[part] = 0.6 * oldp[part] + (1.0 - 0.6) * (
            gram[part, rows_of(y, 64)] + ggot[0, part] + ggot[1, part] + ggot[2, part]
        )
        here, there = columns[n].at[x * 2 + zh], sall.at[half, part, y]
        halved.append(net.push(piece.at[part], there, half=1))
        for late in ((0,), (), (1, 2))[n]:
            across[late] = net.push(piece.at[SETS[late]], columns[late].at[x * 2 + zh], zh=1)
        first_up.append(net.push(piece.at[part], here, x=1))
        first_down.append(net.push(piece.at[part], here, x=3))
        y_up.append(net.push(piece.at[part], there, y=1))
        y_down.append(net.push(piece.at[part], there, y=3))
        own.append(net.move(piece.at[part], here))
        own_piece.append(net.move(piece.at[part], there))

    first_far, second_up, second_down, second_far = [], [], [], []

    def pass_first(n):
        first_up[n].wait_recv()
        there = columns[n].at[back * 2 + zh]
        first_far.append(net.push(there, there, x=1))

    def start_second(n):
        across[n].wait_recv()
        there = columns[n].at[x * 2 + 1 - zh]
        second_down.append(net.push(there, there, x=3))
        second_up.append(net.push(there, there, x=1))

    def pass_second(n):
        second_down[n].wait_recv()
        there = columns[n].at[on * 2 + 1 - zh]
        second_far.append(net.push(there, there, x=3))

    def choose(n):
        own[n].wait()
        for copy in (first_down[n], first_far[n], second_up[n], second_far[n]):
            copy.wait_recv()
        swapped = {}
        for k in (2, 1, 3, 0):
            index, mask = slot_away[k]
            leave[n][k] = columns[n][index] * mask
            swapped[k] = net.push(leave[n].at[k], enter[n].at[k], c=1)
        sent = {}
        for k in (2, 1, 3, 0):
            index, mask = slot_home[k]
            ready[n][k] = columns[n][index] * mask
            swapped[k].wait_recv()
            ready[n][k] = ready[n][k] + enter[n][k]
            here = parts.at[SETS[n], y]
            if k:
                sent[k] = net.push(ready[n].at[k], here, y=k)
            else:
                kept = net.move(ready[n].at[0], here)
        return sent, kept

    def pass_own(n):
        y_up[n].wait_recv()
        there = sall.at[half, SETS[n], below]
        y_far.append(net.push(there, there, y=1))

    def start_other(n):
        halved[n].wait_recv()
        there = sall.at[1 - half, SETS[n], y]
        other_down.append(net.push(there, there, y=3))
        other_up.append(net.push(there, there, y=1))

    def pass_other(n):
        other_down[n].wait_recv()
        there = sall.at[1 - half, SETS[n], above]
        other_far.append(net.push(there, there, y=3))

    pass_first(0)
    pass_own(0)
    start_other(0)
    start_second(0)
    pass_first(1)
    pass_own(1)
    start_other(1)
    pass_second(0)
    pass_other(0)
    pass_first(2)
    pass_own(2)
    start_second(1)
    start_other(2)
    pass_other(1)
    sent = [choose(0)]
    pass_second(1)
    start_second(2)
    pass_other(2)
    sent.append(choose(1))
    pass_second(2)

    halves = []
    for k in (0, 1, 3, 2):
        if k:
            sent[0][0][k].wait_recv()
        else:
            sent[0][1].wait()
        at = (y + 4 - k) % 4
        halves.append(net.push(parts.at[SETS[0], at], crossed.at[:, at], half=1))

    for n in range(3):
        own_piece[n].wait()
        for copy in (y_down[n], y_far[n], other_up[n], other_far[n]):
            copy.wait_recv()
    for h in range(2):
        for n in range(5):
            i, j = PACKED[h][n]
            stat[pl.ds(i * 256, 256), pl.ds(j * 256, 256)] = sall[h, n].reshape(256, 256)
    for i, j in ((0, 1), (0, 2), (0, 3), (2, 1), (3, 1), (2, 3)):
        stat[pl.ds(j * 256, 256), pl.ds(i * 256, 256)] = stat[pl.ds(i * 256, 256), pl.ds(j * 256, 256)].T
    top = top_value(stat, column)
    sent.append(choose(2))
    find_root((y, zl), top, stat, rootbuf, base, high, low)
    returned = net.push(rootbuf.at[1], roots.at[side], side=1)
    kept = net.move(rootbuf.at[0], roots.at[side])

    for n in (1, 2):
        sent[n][1].wait()
        for k in (1, 3, 2):
            sent[n][0][k].wait_recv()
    for copy in halves:
        copy.wait_recv()

    def put(i, j, values):
        rows, cols = pl.ds(i * 256, 256), pl.ds(j * 256, 256)
        new[rows, cols] = new[rows, cols] + values

    def part(n):
        return parts[n].reshape(256, 256)

    def turned_part(n):
        return crossed[n].reshape(256, 256).T

    @pl.when(half == 0)
    def _():
        put(0, 0, part(2))
        put(0, 1, part(3))
        put(0, 2, part(0))
        put(0, 3, part(1))
        put(1, 0, part(3).T)
        put(1, 1, part(4))
        put(1, 2, turned_part(0))
        put(1, 3, turned_part(1))

    @pl.when(half == 1)
    def _():
        put(0, 0, turned_part(0))
        put(0, 1, part(0))
        put(0, 2, part(2))
        put(0, 3, part(3))
        put(1, 0, turned_part(1))
        put(1, 1, part(1))
        put(1, 2, part(3).T)
        put(1, 3, part(4))

    written = net.move(new, new_out)
    kept.wait()
    returned.wait_recv()
    written.wait()
    net.close()


def f32(*shape):
    return jax.ShapeDtypeStruct(shape, jnp.float32)


def refresh(owner, grads, old):
    strips, rows = (GROUPS, 4, SUB, BS), (GROUPS, 2, SUB, BS)
    piece = (5, 64, 256)
    scratch = [strips, strips, strips, strips, (GROUPS, 2, 2, SUB, BS), rows, rows, (GROUPS, SUB, BS)]
    scratch += [(2, 64, BS), (2, 64, BS), (4, 64, BS), (5, 256, 256), (4, *piece), piece]
    scratch += [(2, GROUPS, 4, SUB, 256), (4, 4, 64, 256), (5, 256, 256), (3, *piece), (2, 5, 4, 64, 256)]
    scratch += [(BS, BS), (BS, 1), (BS, BS), (2, 64, BS)]
    scratch += [piece, (5, 4, 64, 256), (2, 4, 64, 256), (512, BS)]
    for count in (16, 8, 8, 8, 4, 4):
        scratch += [(count, part.size, 16, 256) for part in OLD_SETS]
    for count in (8, 4, 4, 4):
        scratch += [(count, part.size, 64, 256) for part in SETS]
    halves = [(4, 256, 256), (4, 256, 256), (BS, BS), (BS, BS)]
    out_shape = (f32(512, BS), f32(2, 64, BS))
    return pl.pallas_call(
        refresh_kernel,
        out_shape=out_shape,
        in_specs=[pl.BlockSpec(memory_space=pltpu.SMEM)] + [pl.BlockSpec(memory_space=pl.ANY)] * 2,
        out_specs=tuple(pl.BlockSpec(memory_space=pl.ANY) for _ in out_shape),
        scratch_shapes=[pltpu.VMEM(shape, jnp.float32) for shape in scratch]
        + [pltpu.VMEM(shape, jnp.bfloat16) for shape in halves]
        + [
            pltpu.SemaphoreType.DMA((256,)),
            pltpu.SemaphoreType.DMA((256,)),
            pltpu.SemaphoreType.DMA((64,)),
        ],
        compiler_params=pltpu.CompilerParams(
            collective_id=0, has_side_effects=True, vmem_limit_bytes=VMEM_LIMIT
        ),
    )(owner, grads, old)


def per_device(grads, owner, stats):
    new, roots = refresh(owner, grads.reshape(4, 4, 64, BS), stats[0, 0])
    return new[None, None], roots[None]


def solution(mesh):
    return jax.shard_map(
        per_device,
        mesh=mesh,
        in_specs=(P("dp", "block", None, None), P(), P("block", "dp", None, None)),
        out_specs=(P("block", "dp", None, None), P("block", None, "dp", None)),
        check_vma=False,
    )
```
